256 devices in a mesh: ctx: 64 (over z, x, core), head: 4 (over y).
Axes of the slice: x: 4, y: 4, z: 8, core: 2. Of those that a mesh axis runs over, the one named last changes fastest.
Arguments:
- query_raw: bfloat16 [65536, 4096], P('ctx', 'head'), may hold values from -6 to 6
- key_raw: bfloat16 [65536, 4096], P('ctx', 'head'), may hold values from -6 to 6
- value_raw: bfloat16 [65536, 4096], P('ctx', 'head'), may hold values from -6 to 6
- gate_raw: bfloat16 [65536, 4096], P('ctx', 'head'), may hold values from -6 to 6
- conv_weight: float32 [3, 4, 4096], P(None, None, 'head'), as said below
- norm_gain: float32 [4096], P('head'), may hold values from 0.1 to 1.9
Outputs:
- attended: bfloat16 [65536, 4096], P('ctx', 'head')
The draws below stay inside these ranges and needn't reach their ends.
Inputs may be any that keep to these rules, and one draw needn't show every extreme that they name: `conv_weight`: taps of the short convolutions.
All inputs are finite; a program needn't handle non-finite values.
Results may differ from the reference program's by a relative error of at most 0.0061.
Values may be sent and summed in bfloat16 or wider, within the bound.
A program may use at most 128 MiB of HBM per device.

```python
import jax
import jax.numpy as jnp
from jax import lax

HEADS = 32
DH = 128
KW = 4
BLOCK = 512
TOKENS = 65536


def draw_conv_weight(key, part):
    key = jax.random.fold_in(key, 7)
    channels = HEADS * DH
    base_draw = 0.5 * jax.random.normal(key, (3, KW, channels), jnp.float32)
    position = jnp.arange(channels, dtype=jnp.float32) / (channels - 1)
    rising = 3.0 ** position
    steady = jnp.ones((channels,), jnp.float32)
    col_scale = jnp.stack([steady, steady, rising])[:, None, :]
    return base_draw * col_scale


def shard_levels(key, extent, cuts, smallest, top_value):
    def one(dim, blocks):
        heights = jax.random.uniform(jax.random.fold_in(jax.random.fold_in(key, 6), dim), (blocks,), jnp.float32, smallest / len(cuts), top_value / len(cuts))
        return jnp.repeat(jnp.exp(heights), extent[dim] // blocks).reshape((-1,) + (1,) * (len(extent) - dim - 1))

    level = one(*cuts[0])
    for cut in cuts[1:]:
        level = level * one(*cut)
    return level


def centred(key, shape, spread, bound, cuts=(), kind=jnp.bfloat16):
    values = spread * jax.random.normal(key, shape, jnp.float32)
    if cuts:
        values = values * shard_levels(key, shape, cuts, -0.22, 0.18)
    return jnp.clip(values, -bound, bound).astype(kind)


def setup_inputs(seed: int = 0) -> dict:
    key_of = jax.random.split(jax.random.key(seed), 7)
    query_raw = centred(key_of[0], (TOKENS, HEADS * DH), 1.0, 6.0, ((0, 64), (1, 4)))
    key_raw = centred(key_of[1], (TOKENS, HEADS * DH), 1.0, 6.0, ((0, 64), (1, 4)))
    value_raw = centred(key_of[2], (TOKENS, HEADS * DH), 1.0, 6.0, ((0, 64), (1, 4)))
    gate_raw = centred(key_of[3], (TOKENS, HEADS * DH), 1.0, 6.0, ((0, 64), (1, 4)))
    conv_weight = draw_conv_weight(jax.random.fold_in(key_of[6], 71), 0)
    norm_gain = jnp.clip(1.0 + 0.18 * jax.random.normal(key_of[5], (HEADS * DH,), jnp.float32), 0.1, 1.9)
    return {"query_raw": query_raw, "key_raw": key_raw, "value_raw": value_raw, "gate_raw": gate_raw, "conv_weight": conv_weight, "norm_gain": norm_gain}


def rounded(value):
    return lax.optimization_barrier(value.astype(jnp.bfloat16)).astype(jnp.float32)

def reference(query_raw, key_raw, value_raw, gate_raw, conv_weight, norm_gain):
    channels = HEADS * DH
    block_count = TOKENS // BLOCK
    rim_rows = KW - 1
    blocked = tuple((item.reshape(block_count, BLOCK, channels) for item in (query_raw, key_raw, value_raw, gate_raw)))
    causal = jnp.arange(BLOCK)[:, None] >= jnp.arange(BLOCK)[None, :]
    high = lax.Precision.HIGHEST

    def advance(carry, pieces):
        state, tails = carry
        query_blk, key_blk, value_blk, gate_blk = pieces
        raws = jnp.stack([query_blk, key_blk, value_blk]).astype(jnp.float32)
        extended = jnp.concatenate([tails, raws], axis=1)
        conved = conv_weight[:, 0][:, None, :] * extended[:, 0:BLOCK]
        for offset in range(1, KW):
            conved = conved + conv_weight[:, offset][:, None, :] * extended[:, offset:offset + BLOCK]
        queries = rounded(jax.nn.silu(conved[0]) * DH ** (-0.5)).reshape(BLOCK, HEADS, DH)
        keys_bf = rounded(jax.nn.silu(conved[1])).reshape(BLOCK, HEADS, DH)
        values_bf = rounded(conved[2]).reshape(BLOCK, HEADS, DH)
        scores = jnp.einsum('qhd,khd->hqk', queries, keys_bf, precision=high)
        weights = rounded(jnp.where(causal[None], scores, 0.0))
        inner = jnp.einsum('hqk,khd->qhd', weights, values_bf, precision=high)
        outer = jnp.einsum('qhd,hde->qhe', queries, rounded(state), precision=high)
        mixed = (inner + outer).reshape(BLOCK, channels)
        square = lax.optimization_barrier(jnp.sum(mixed * mixed, axis=1, keepdims=True))
        output = mixed * lax.rsqrt(square / channels + 1e-06) * norm_gain[None, :] * jax.nn.sigmoid(gate_blk.astype(jnp.float32))
        state = state + jnp.einsum('khd,khe->hde', keys_bf, values_bf, precision=high)
        tails = raws[:, BLOCK - rim_rows:]
        return ((state, tails), output.astype(jnp.bfloat16))
    start_state = jnp.zeros((HEADS, DH, DH), jnp.float32)
    start_tails = jnp.zeros((3, rim_rows, channels), jnp.float32)
    carry, outputs = lax.scan(advance, (start_state, start_tails), blocked)
    return outputs.reshape(TOKENS, channels)
```

```python
import functools

import jax
import jax.numpy as jnp
from jax import lax
from jax.experimental import pallas as pl
from jax.experimental.pallas import tpu as pltpu
from jax.sharding import PartitionSpec as P

DH = 128
KW = 4
CHUNK = 256
STRIP = 64
TILE = 16
SLAB = 8
PAIR = 2
MESH = pl.DeviceIdType.MESH


def conv_rows(extended, taps):
    behind = pltpu.roll(extended, 1, 0)
    near = taps[3] * extended + taps[2] * behind
    far = taps[1] * extended + taps[0] * behind
    return (near + pltpu.roll(far, 2, 0))[8:]


def kernel(
    sizes,
    q_hbm,
    k_hbm,
    v_hbm,
    g_hbm,
    taps_ref,
    gain_ref,
    out_hbm,
    raw,
    cooked,
    halo,
    mixed,
    gates,
    part_state,
    send_slices,
    recv_slices,
    before,
    send_total,
    recv_total,
    send_prefix,
    prefix,
    send_square,
    recv_square,
    out_buf,
    load_sem,
    halo_send_sem,
    halo_recv_sem,
    slice_send_sem,
    slice_recv_sem,
    total_send_sem,
    total_recv_sem,
    prefix_send_sem,
    prefix_recv_sem,
    square_send_sem,
    square_recv_sem,
    store_sem,
):
    heads, tokens, slabs, ranks = sizes
    channels = heads * DH
    chunks = tokens // CHUNK
    groups = heads // PAIR
    ctx = lax.axis_index("ctx")
    rank = lax.axis_index("head")
    slab = ctx // SLAB
    place = lax.rem(ctx, SLAB)
    ctx_count = slabs * SLAB

    sources = (k_hbm, v_hbm, q_hbm, g_hbm)

    def load(array, head):
        return pltpu.make_async_copy(
            sources[array].at[:, pl.ds(pl.multiple_of(head * DH, DH), DH)],
            raw.at[array, head],
            load_sem.at[array, head],
        )

    barrier = pltpu.get_barrier_semaphore()

    def greet(target_ctx, target_rank):
        pl.semaphore_signal(
            barrier, inc=1, device_id=(target_ctx, target_rank), device_id_type=MESH
        )

    for head in range(heads):
        load(0, head).start()
        load(1, head).start()

    for step in range(1, SLAB):
        greet(slab * SLAB + lax.rem(place + step, SLAB), rank)
    for step in range(1, slabs):
        greet(lax.rem(slab + step, slabs) * SLAB + place, rank)
    for step in range(1, ranks):
        greet(ctx, lax.rem(rank + step, ranks))

    greet(lax.rem(ctx + 1, ctx_count), rank)
    greet(lax.rem(ctx + ctx_count - 1, ctx_count), rank)

    for head in range(heads):
        load(2, head).start()
    for head in range(heads):
        load(3, head).start()

    pl.semaphore_wait(barrier, SLAB - 1 + slabs - 1 + ranks - 1 + 2)

    def halo_copy(array):
        return pltpu.make_async_remote_copy(
            src_ref=sources[array].at[pl.ds(tokens - TILE, TILE), :],
            dst_ref=halo.at[array],
            send_sem=halo_send_sem.at[array],
            recv_sem=halo_recv_sem.at[array],
            device_id=(ctx + 1, rank),
            device_id_type=MESH,
        )

    @pl.when(ctx < ctx_count - 1)
    def _():
        for array in range(3):
            halo_copy(array).start()

    @pl.when(ctx == 0)
    def _():
        halo[...] = jnp.zeros_like(halo)

    def halo_wait(array):
        @pl.when(ctx > 0)
        def _():
            halo_copy(array).wait_recv()

    def lanes(head):
        return pl.ds(pl.multiple_of(head * DH, DH), DH)

    def taps_of(kind, head, factor):
        return [taps_ref[kind, j : j + 1, lanes(head)] * factor for j in range(KW)]

    def extended_rows(array, head, row):
        if row == 0:
            ahead = halo[array, :, lanes(head)]
            own = raw[array, head, 0:STRIP, :]
            return jnp.concatenate(
                [ahead.astype(jnp.float32)[8:], own.astype(jnp.float32)], axis=0
            )
        return raw[array, head, row - TILE : row + STRIP, :].astype(jnp.float32)[8:]

    def keys_values(head, chunk):
        key_taps = taps_of(1, head, 0.5)
        value_taps = taps_of(2, head, 1.0)
        first = chunk * CHUNK
        for row in range(first, first + CHUNK, STRIP):
            half = conv_rows(extended_rows(0, head, row), key_taps)
            cooked[0, head, row : row + STRIP, :] = (half + half * jnp.tanh(half)).astype(
                jnp.bfloat16
            )
            cooked[1, head, row : row + STRIP, :] = conv_rows(
                extended_rows(1, head, row), value_taps
            ).astype(jnp.bfloat16)
        part_state[head, chunk] = lax.dot_general(
            cooked[0, head, first : first + CHUNK, :],
            cooked[1, head, first : first + CHUNK, :],
            (((0,), (0,)), ((), ())),
            preferred_element_type=jnp.float32,
        )

    def finish_state(head, group, member):
        running = part_state[head, 0]
        for chunk in range(1, chunks):
            own = part_state[head, chunk]
            part_state[head, chunk] = running
            running = running + own
        part_state[head, 0] = jnp.zeros((DH, DH), jnp.float32)
        rounded = running.astype(jnp.bfloat16)
        for piece in range(SLAB):
            send_slices[group, piece, member] = rounded[piece * TILE : (piece + 1) * TILE]

    def peer(step):
        return lax.rem(place + step, SLAB)

    def slice_copy(group, step):
        return pltpu.make_async_remote_copy(
            src_ref=send_slices.at[group, peer(step)],
            dst_ref=recv_slices.at[group, step - 1],
            send_sem=slice_send_sem.at[group],
            recv_sem=slice_recv_sem.at[group],
            device_id=(slab * SLAB + peer(step), rank),
            device_id_type=MESH,
        )

    def total_copy(group, other):
        return pltpu.make_async_remote_copy(
            src_ref=send_total.at[group],
            dst_ref=recv_total.at[group, slab],
            send_sem=total_send_sem.at[group, other],
            recv_sem=total_recv_sem.at[group, slab],
            device_id=(other * SLAB + place, rank),
            device_id_type=MESH,
        )

    def total_arrival(group, other):
        return pltpu.make_async_remote_copy(
            src_ref=send_total.at[group],
            dst_ref=recv_total.at[group, other],
            send_sem=total_send_sem.at[group, other],
            recv_sem=total_recv_sem.at[group, other],
            device_id=(other * SLAB + place, rank),
            device_id_type=MESH,
        )

    def prefix_copy(group, step):
        return pltpu.make_async_remote_copy(
            src_ref=send_prefix.at[group, peer(step)],
            dst_ref=prefix.at[group, place],
            send_sem=prefix_send_sem.at[group],
            recv_sem=prefix_recv_sem.at[group],
            device_id=(slab * SLAB + peer(step), rank),
            device_id_type=MESH,
        )

    def whole(ref, sem):
        return pltpu.make_async_copy(ref, ref, sem)

    def send_states(group):
        for step in range(1, SLAB):
            slice_copy(group, step).start()

    def sum_slab(group):
        whole(recv_slices.at[group], slice_recv_sem.at[group]).wait()
        total = send_slices[group, place].astype(jnp.float32)
        for step in range(1, SLAB):
            total = total + recv_slices[group, step - 1].astype(jnp.float32)
        send_total[group] = total.astype(jnp.bfloat16)
        for other in range(1, slabs):

            @pl.when(other > slab)
            def _():
                total_copy(group, other).start()

        running = jnp.zeros((PAIR, TILE, DH), jnp.float32)
        for index in range(SLAB):
            before[group, index] = running
            if index < SLAB - 1:
                step = lax.rem(place - index + SLAB, SLAB)
                got = recv_slices[group, jnp.maximum(step - 1, 0)].astype(jnp.float32)
                own = send_slices[group, place].astype(jnp.float32)
                running = running + jnp.where(step == 0, own, got)

    def send_prefixes(group):
        def add(other, total):
            total_arrival(group, other).wait_recv()
            return total + recv_total[group, other].astype(jnp.float32)

        earlier = lax.fori_loop(0, slab, add, jnp.zeros((PAIR, TILE, DH), jnp.float32))
        for index in range(SLAB):
            send_prefix[group, index] = (earlier + before[group, index]).astype(jnp.bfloat16)
        for step in range(1, SLAB):
            prefix_copy(group, step).start()
        prefix[group, place] = send_prefix[group, place]

    def queries(head):
        query_taps = taps_of(0, head, 0.5)
        for row in range(0, tokens, STRIP):
            half = conv_rows(extended_rows(2, head, row), query_taps)
            scaled = half * DH ** (-0.5)
            cooked[2, head, row : row + STRIP, :] = (scaled + scaled * jnp.tanh(half)).astype(
                jnp.bfloat16
            )

    def inner(head):
        token = lax.broadcasted_iota(jnp.int32, (CHUNK, CHUNK), 0)
        source = lax.broadcasted_iota(jnp.int32, (CHUNK, CHUNK), 1)
        for chunk in range(chunks):
            rows = pl.ds(chunk * CHUNK, CHUNK)
            scores = lax.dot_general(
                cooked[2, head, rows, :],
                cooked[0, head, rows, :],
                (((1,), (1,)), ((), ())),
                preferred_element_type=jnp.float32,
            )
            weights = jnp.where(token >= source, scores, 0.0).astype(jnp.bfloat16)
            mixed[head, rows, :] = jnp.dot(
                weights, cooked[1, head, rows, :], preferred_element_type=jnp.float32
            )

    def gate(head):
        gain = gain_ref[pl.ds(head, 1), :] * 0.5
        for row in range(0, tokens, STRIP):
            half = raw[3, head, row : row + STRIP, :].astype(jnp.float32) * 0.5
            gates[head, row : row + STRIP, :] = gain + gain * jnp.tanh(half)

    def loop(first, last, body):
        def step(index, _):
            body(index)
            return 0

        lax.fori_loop(first, last, step, 0)

    early = heads // 2

    def later_chunks(head):
        load(0, head).wait()
        load(1, head).wait()
        for chunk in range(1, chunks):
            keys_values(head, chunk)

    loop(0, early, later_chunks)
    halo_wait(0)
    halo_wait(1)
    for group in range(groups):
        def whole_head(head):
            @pl.when(head >= early)
            def _():
                later_chunks(head)
            keys_values(head, 0)
            finish_state(head, group, head - group * PAIR)

        loop(group * PAIR, (group + 1) * PAIR, whole_head)
        send_states(group)

    halo_wait(2)

    def query_part(head):
        load(2, head).wait()
        load(3, head).wait()
        queries(head)
        inner(head)
        gate(head)

    loop(0, 1, query_part)
    sum_slab(0)
    sum_slab(1)
    loop(1, 2, query_part)
    sum_slab(2)
    loop(2, 3, query_part)
    sum_slab(3)
    loop(3, 4, query_part)
    send_prefixes(0)
    send_prefixes(1)
    loop(4, 5, query_part)
    send_prefixes(2)
    loop(5, 6, query_part)
    send_prefixes(3)
    loop(6, 8, query_part)

    for group in range(groups):
        whole(recv_slices.at[group], prefix_recv_sem.at[group]).wait()

    eye = (
        lax.broadcasted_iota(jnp.int32, (128, 128), 0)
        == lax.broadcasted_iota(jnp.int32, (128, 128), 1)
    )

    def square_copy(chunk, step):
        return pltpu.make_async_remote_copy(
            src_ref=send_square.at[chunk],
            dst_ref=recv_square.at[chunk, step - 1],
            send_sem=square_send_sem.at[chunk],
            recv_sem=square_recv_sem.at[chunk],
            device_id=(ctx, lax.rem(rank + step, ranks)),
            device_id_type=MESH,
        )

    def outer(chunk):
        rows = pl.ds(chunk * CHUNK, CHUNK)

        def add_head(head, squares):
            carried = prefix[head // PAIR, :, lax.rem(head, PAIR)].reshape(DH, DH)
            state = (carried.astype(jnp.float32) + part_state[head, chunk]).astype(jnp.bfloat16)
            here = mixed[head, rows, :] + jnp.dot(
                cooked[2, head, rows, :], state, preferred_element_type=jnp.float32
            )
            mixed[head, rows, :] = here * gates[head, rows, :]
            return squares + here * here

        squares = lax.fori_loop(0, heads, add_head, jnp.zeros((CHUNK, DH), jnp.float32))
        column = jnp.sum(squares, axis=1, keepdims=True)
        for part in range(CHUNK // 128):
            send_square[chunk, part : part + 1, :] = jnp.sum(
                jnp.where(eye, column[part * 128 : (part + 1) * 128], 0.0), axis=0, keepdims=True
            )
        for step in range(1, ranks):
            square_copy(chunk, step).start()

    def store(chunk):
        return pltpu.make_async_copy(
            out_buf.at[pl.ds(chunk * CHUNK, CHUNK), :],
            out_hbm.at[pl.ds(chunk * CHUNK, CHUNK), :],
            store_sem.at[chunk],
        )

    def finish(chunk):
        whole(recv_square.at[chunk], square_recv_sem.at[chunk]).wait()
        square = send_square[chunk, 0 : CHUNK // 128]
        for step in range(1, ranks):
            square = square + recv_square[chunk, step - 1, 0 : CHUNK // 128]
        factor = lax.rsqrt(square / (channels * ranks) + 1e-06)
        for part in range(CHUNK // 128):
            column = jnp.sum(
                jnp.where(eye, factor[part : part + 1], 0.0), axis=1, keepdims=True
            )
            spread = jnp.broadcast_to(column, (128, DH))
            first = chunk * CHUNK + part * 128
            for head in range(heads):
                out_buf[first : first + 128, head * DH : (head + 1) * DH] = (
                    mixed[head, first : first + 128, :] * spread
                ).astype(jnp.bfloat16)
        store(chunk).start()

    for chunk in range(chunks):
        outer(chunk)
        if chunk >= 2:
            finish(chunk - 2)
    finish(chunks - 2)
    finish(chunks - 1)

    for chunk in range(chunks):
        store(chunk).wait()
        whole(recv_square.at[chunk], square_send_sem.at[chunk]).wait()
    for group in range(groups):
        whole(recv_slices.at[group], slice_send_sem.at[group]).wait()
        whole(recv_slices.at[group], prefix_send_sem.at[group]).wait()
        for other in range(1, slabs):

            @pl.when(other > slab)
            def _():
                total_copy(group, other).wait_send()

    @pl.when(ctx < ctx_count - 1)
    def _():
        for array in range(3):
            halo_copy(array).wait_send()


def body(query_raw, key_raw, value_raw, gate_raw, conv_weight, norm_gain):
    tokens, channels = query_raw.shape
    heads = channels // DH
    chunks = tokens // CHUNK
    groups = heads // PAIR
    slabs = lax.axis_size("ctx") // SLAB
    ranks = lax.axis_size("head")
    anywhere = pl.BlockSpec(memory_space=pl.ANY)
    vmem = pl.BlockSpec(memory_space=pltpu.VMEM)
    dma = pltpu.SemaphoreType.DMA
    return pl.pallas_call(
        functools.partial(kernel, (heads, tokens, slabs, ranks)),
        out_shape=jax.ShapeDtypeStruct((tokens, channels), jnp.bfloat16),
        in_specs=[anywhere] * 4 + [vmem] * 2,
        out_specs=anywhere,
        scratch_shapes=[
            pltpu.VMEM((4, heads, tokens, DH), jnp.bfloat16),
            pltpu.VMEM((3, heads, tokens, DH), jnp.bfloat16),
            pltpu.VMEM((3, TILE, channels), jnp.bfloat16),
            pltpu.VMEM((heads, tokens, DH), jnp.float32),
            pltpu.VMEM((heads, tokens, DH), jnp.float32),
            pltpu.VMEM((heads, chunks, DH, DH), jnp.float32),
            pltpu.VMEM((groups, SLAB, PAIR, TILE, DH), jnp.bfloat16),
            pltpu.VMEM((groups, SLAB - 1, PAIR, TILE, DH), jnp.bfloat16),
            pltpu.VMEM((groups, SLAB, PAIR, TILE, DH), jnp.float32),
            pltpu.VMEM((groups, PAIR, TILE, DH), jnp.bfloat16),
            pltpu.VMEM((groups, slabs, PAIR, TILE, DH), jnp.bfloat16),
            pltpu.VMEM((groups, SLAB, PAIR, TILE, DH), jnp.bfloat16),
            pltpu.VMEM((groups, SLAB, PAIR, TILE, DH), jnp.bfloat16),
            pltpu.VMEM((chunks, 8, 128), jnp.float32),
            pltpu.VMEM((chunks, ranks - 1, 8, 128), jnp.float32),
            pltpu.VMEM((tokens, channels), jnp.bfloat16),
            dma((4, heads)),
            dma((3,)),
            dma((3,)),
            dma((groups,)),
            dma((groups,)),
            dma((groups, slabs)),
            dma((groups, slabs)),
            dma((groups,)),
            dma((groups,)),
            dma((chunks,)),
            dma((chunks,)),
            dma((chunks,)),
        ],
        compiler_params=pltpu.CompilerParams(
            collective_id=0, has_side_effects=True, vmem_limit_bytes=56 * 2**20
        ),
    )(
        query_raw,
        key_raw,
        value_raw,
        gate_raw,
        conv_weight,
        norm_gain.reshape(heads, DH),
    )


def solution(mesh):
    placed = (
        P("ctx", "head"),
        P("ctx", "head"),
        P("ctx", "head"),
        P("ctx", "head"),
        P(None, None, "head"),
        P("head"),
    )
    return jax.shard_map(
        body, mesh=mesh, in_specs=placed, out_specs=P("ctx", "head"), check_vma=False
    )
```

```python
import functools

import jax
import jax.numpy as jnp
from jax import lax
from jax.experimental import pallas as pl
from jax.experimental.pallas import tpu as pltpu
from jax.sharding import PartitionSpec as P

DH = 128
KW = 4
CHUNK = 256
STRIP = 64
TILE = 16
SLAB = 8
GROUP = 4
SUBLANES = 8
STRIDE = CHUNK // SUBLANES
HALVES = 2
MESH = pl.DeviceIdType.MESH


def conv_rows(extended, taps):
    behind = pltpu.roll(extended, 1, 0)
    near = taps[3] * extended + taps[2] * behind
    far = taps[1] * extended + taps[0] * behind
    return (near + pltpu.roll(far, 2, 0))[8:]


def kernel(
    sizes,
    q_hbm,
    k_hbm,
    v_hbm,
    g_hbm,
    taps_hbm,
    gain_hbm,
    out_ref,
    raw,
    taps_ref,
    gain_ref,
    cooked,
    tails,
    tail_pack,
    halo,
    stride_order,
    causal,
    mixed,
    gates,
    part_state,
    states,
    squares,
    send_slices,
    recv_slices,
    before,
    send_total,
    recv_total,
    send_prefix,
    prefix,
    send_square,
    recv_square,
    load_sem,
    small_sem,
    tail_sem,
    halo_send_sem,
    halo_recv_sem,
    slice_send_sem,
    slice_recv_sem,
    total_send_sem,
    total_recv_sem,
    prefix_send_sem,
    prefix_recv_sem,
    square_send_sem,
    square_recv_sem,
    ready,
):
    heads, tokens, slabs, ranks = sizes
    channels = heads * DH
    chunks = tokens // CHUNK
    groups = heads // GROUP
    ctx = lax.axis_index("ctx")
    rank = lax.axis_index("head")
    slab = ctx // SLAB
    place = lax.rem(ctx, SLAB)
    ctx_count = slabs * SLAB

    sources = (k_hbm, v_hbm, q_hbm, g_hbm)

    def load(array, head):
        return pltpu.make_async_copy(
            sources[array].at[:, pl.ds(pl.multiple_of(head * DH, DH), DH)],
            raw.at[array, head],
            load_sem.at[array, head],
        )

    barrier = pltpu.get_barrier_semaphore()

    def greet(target_ctx, target_rank):
        pl.semaphore_signal(
            barrier, inc=1, device_id=(target_ctx, target_rank), device_id_type=MESH
        )

    def load_tail(array):
        return pltpu.make_async_copy(
            sources[array].at[pl.ds(tokens - TILE, TILE), :], tails.at[array], tail_sem.at[array]
        )

    load_taps = pltpu.make_async_copy(taps_hbm, taps_ref, small_sem.at[0])
    load_gain = pltpu.make_async_copy(gain_hbm, gain_ref, small_sem.at[1])
    load_taps.start()
    for head in range(2):
        load(0, head).start()
        load(1, head).start()
    for array in range(3):
        load_tail(array).start()
    for head in range(2, heads):
        load(0, head).start()
        load(1, head).start()

    for step in range(1, SLAB):
        greet(slab * SLAB + lax.rem(place + step, SLAB), rank)
    for step in range(1, ranks):
        greet(ctx, lax.rem(rank + step, ranks))

    @pl.when(ctx > 0)
    def _():
        greet(ctx - 1, rank)

    @pl.when(ctx < ctx_count - 1)
    def _():
        greet(ctx + 1, rank)

    for other in range(1, slabs):

        @pl.when(other > slab)
        def _():
            greet(other * SLAB + place, rank)

    load_gain.start()
    for head in range(heads):
        load(2, head).start()
        load(3, head).start()

    row = lax.broadcasted_iota(jnp.int32, (CHUNK, CHUNK), 0)
    column = lax.broadcasted_iota(jnp.int32, (CHUNK, CHUNK), 1)

    def token_of(position):
        return position % SUBLANES * STRIDE + position // SUBLANES

    stride_order[...] = jnp.where(column == token_of(row), 1.0, 0.0).astype(jnp.bfloat16)
    causal[...] = jnp.where(row >= token_of(column), 1.0, 0.0).astype(jnp.bfloat16)

    halo_copy = pltpu.make_async_remote_copy(
        src_ref=tail_pack,
        dst_ref=halo,
        send_sem=halo_send_sem,
        recv_sem=halo_recv_sem,
        device_id=(ctx + 1, rank),
        device_id_type=MESH,
    )

    def lanes(head):
        return slice(head * DH, (head + 1) * DH)

    def taps_of(kind, head, factor):
        return [taps_ref[kind, j : j + 1, lanes(head)] * factor for j in range(KW)]

    first_sublane = lax.broadcasted_iota(jnp.int32, (SUBLANES, DH), 0) == 0

    def conv_strided(rows, ahead, taps):
        edge = [
            jnp.where(
                first_sublane,
                ahead[j],
                pltpu.roll(rows[CHUNK + (j - 3) * SUBLANES :][:SUBLANES], 1, 0),
            )
            for j in range(KW - 1)
        ]
        extended = jnp.concatenate(edge + [rows], axis=0)
        terms = [
            taps[j] * extended[j * SUBLANES : j * SUBLANES + CHUNK] for j in range(KW)
        ]
        return (terms[3] + terms[2]) + (terms[1] + terms[0])

    def last_rows(rows):
        return [
            pltpu.roll(rows[CHUNK + (j - 3) * SUBLANES :][:SUBLANES], 1, 0) for j in range(KW - 1)
        ]

    def in_stride_order(array, pair, chunk):
        rows = slice(chunk * CHUNK, (chunk + 1) * CHUNK)
        both = jnp.concatenate([raw[array, 2 * pair, rows], raw[array, 2 * pair + 1, rows]], axis=1)
        return jnp.dot(stride_order[...], both, preferred_element_type=jnp.float32)

    def keys_values(pair, chunk, rows_of, ahead_of):
        for member in range(2):
            head = 2 * pair + member
            here = slice(member * DH, (member + 1) * DH)
            rows = slice(chunk * CHUNK, (chunk + 1) * CHUNK)
            half = conv_strided(rows_of[0][:, here], ahead_of(0, member), taps_of(1, head, 0.5))
            cooked[0, head, rows] = (half + half * jnp.tanh(half)).astype(jnp.bfloat16)
            cooked[1, head, rows] = conv_strided(
                rows_of[1][:, here], ahead_of(1, member), taps_of(2, head, 1.0)
            ).astype(jnp.bfloat16)

    def later_chunks(pair):
        previous = [in_stride_order(array, pair, 0) for array in range(2)]
        for chunk in range(1, chunks):
            behind = [last_rows(item) for item in previous]

            def ahead_of(array, member):
                return [item[:, member * DH : (member + 1) * DH] for item in behind[array]]

            previous = [in_stride_order(array, pair, chunk) for array in range(2)]
            keys_values(pair, chunk, previous, ahead_of)

    def first_chunk(pair):
        def ahead_of(array, member):
            head = 2 * pair + member
            rows = halo[:, lanes(head)].astype(jnp.float32)
            return [rows[array * 3 + j : array * 3 + j + 1] for j in range(KW - 1)]

        keys_values(pair, 0, [in_stride_order(array, pair, 0) for array in range(2)], ahead_of)

    def product(head, chunk):
        rows = slice(chunk * CHUNK, (chunk + 1) * CHUNK)
        part_state[head, chunk] = lax.dot_general(
            cooked[0, head, rows],
            cooked[1, head, rows],
            (((0,), (0,)), ((), ())),
            preferred_element_type=jnp.float32,
        )

    def pack_tails():
        wide = lax.broadcasted_iota(jnp.int32, (TILE, channels), 0)
        key, value, query = [
            pltpu.roll(tails[array].astype(jnp.float32), 3 * (array + 1), 0) for array in range(3)
        ]
        packed = jnp.where(wide < 3, key, jnp.where(wide < 6, value, query))
        tail_pack[...] = packed.astype(jnp.bfloat16)

    def extended_rows(array, head, row):
        if row == 0:
            ahead = halo[:, lanes(head)].astype(jnp.float32)
            own = raw[array, head, 0:STRIP, :]
            return jnp.concatenate(
                [pltpu.roll(ahead, TILE - 1, 0)[:SUBLANES], own.astype(jnp.float32)], axis=0
            )
        return raw[array, head, row - TILE : row + STRIP, :].astype(jnp.float32)[8:]

    def finish_state(head, group, member):
        running = part_state[head, 0]
        for chunk in range(1, chunks):
            own = part_state[head, chunk]
            part_state[head, chunk] = running
            running = running + own
        part_state[head, 0] = jnp.zeros((DH, DH), jnp.float32)
        rounded = running.astype(jnp.bfloat16)
        for piece in range(SLAB):
            send_slices[group, piece, member] = rounded[piece * TILE : (piece + 1) * TILE]

    def peer(step):
        return lax.rem(place + step, SLAB)

    def slice_copy(group, step):
        return pltpu.make_async_remote_copy(
            src_ref=send_slices.at[group, peer(step)],
            dst_ref=recv_slices.at[group, step - 1],
            send_sem=slice_send_sem.at[group],
            recv_sem=slice_recv_sem.at[group],
            device_id=(slab * SLAB + peer(step), rank),
            device_id_type=MESH,
        )

    def total_copy(group, other):
        return pltpu.make_async_remote_copy(
            src_ref=send_total.at[group],
            dst_ref=recv_total.at[group, slab],
            send_sem=total_send_sem.at[group, other],
            recv_sem=total_recv_sem.at[group, slab],
            device_id=(other * SLAB + place, rank),
            device_id_type=MESH,
        )

    def total_arrival(group, other):
        return pltpu.make_async_remote_copy(
            src_ref=send_total.at[group],
            dst_ref=recv_total.at[group, other],
            send_sem=total_send_sem.at[group, other],
            recv_sem=total_recv_sem.at[group, other],
            device_id=(other * SLAB + place, rank),
            device_id_type=MESH,
        )

    def prefix_copy(group, step):
        return pltpu.make_async_remote_copy(
            src_ref=send_prefix.at[group, peer(step)],
            dst_ref=prefix.at[group, place],
            send_sem=prefix_send_sem.at[group],
            recv_sem=prefix_recv_sem.at[group],
            device_id=(slab * SLAB + peer(step), rank),
            device_id_type=MESH,
        )

    def whole(ref, sem):
        return pltpu.make_async_copy(ref, ref, sem)

    def send_states(group):
        for step in range(1, SLAB):
            slice_copy(group, step).start()

    def sum_slab(group):
        whole(recv_slices.at[group], slice_recv_sem.at[group]).wait()
        total = send_slices[group, place].astype(jnp.float32)
        for step in range(1, SLAB):
            total = total + recv_slices[group, step - 1].astype(jnp.float32)
        send_total[group] = total.astype(jnp.bfloat16)
        if group == 0:

            @pl.when(slab < slabs - 1)
            def _():
                pl.semaphore_wait(ready, slabs - 1 - slab)

        for other in range(1, slabs):

            @pl.when(other > slab)
            def _():
                total_copy(group, other).start()

        running = jnp.zeros((GROUP, TILE, DH), jnp.float32)
        for index in range(SLAB):
            before[group, index] = running
            if index < SLAB - 1:
                step = lax.rem(place - index + SLAB, SLAB)
                got = recv_slices[group, jnp.maximum(step - 1, 0)].astype(jnp.float32)
                own = send_slices[group, place].astype(jnp.float32)
                running = running + jnp.where(step == 0, own, got)

    def send_prefixes(group):
        def add(other, total):
            total_arrival(group, other).wait_recv()
            return total + recv_total[group, other].astype(jnp.float32)

        earlier = lax.fori_loop(0, slab, add, jnp.zeros((GROUP, TILE, DH), jnp.float32))
        for index in range(SLAB):
            send_prefix[group, index] = (earlier + before[group, index]).astype(jnp.bfloat16)
        for step in range(1, SLAB):
            prefix_copy(group, step).start()
        prefix[group, place] = send_prefix[group, place]

    def queries(head):
        query_taps = taps_of(0, head, 0.5)
        for row in range(0, tokens, STRIP):
            half = conv_rows(extended_rows(2, head, row), query_taps)
            scaled = half * DH ** (-0.5)
            cooked[2, head, row : row + STRIP, :] = (scaled + scaled * jnp.tanh(half)).astype(
                jnp.bfloat16
            )

    def inner(head):
        for chunk in range(chunks):
            rows = slice(chunk * CHUNK, (chunk + 1) * CHUNK)
            scores = lax.dot_general(
                cooked[2, head, rows],
                cooked[0, head, rows],
                (((1,), (1,)), ((), ())),
                preferred_element_type=jnp.float32,
            )
            weights = scores.astype(jnp.bfloat16) * causal[...]
            mixed[head, rows] = jnp.dot(
                weights, cooked[1, head, rows], preferred_element_type=jnp.float32
            )

    def gate(head):
        gain = gain_ref[pl.ds(head, 1), :] * 0.5
        for row in range(0, tokens, STRIP):
            half = raw[3, head, row : row + STRIP, :].astype(jnp.float32) * 0.5
            gates[head, row : row + STRIP, :] = gain + gain * jnp.tanh(half)

    pairs = heads // 2

    def pair_loads(array, pair):
        load(array, 2 * pair).wait()
        load(array, 2 * pair + 1).wait()

    load_taps.wait()
    for pair in range(pairs // 2):
        pair_loads(0, pair)
        pair_loads(1, pair)
        later_chunks(pair)

    for array in range(3):
        load_tail(array).wait()
    pack_tails()
    pl.semaphore_wait(
        barrier,
        SLAB - 1 + ranks - 1 + slab + jnp.minimum(ctx, 1) + jnp.minimum(ctx_count - 1 - ctx, 1),
    )

    @pl.when(ctx < ctx_count - 1)
    def _():
        halo_copy.start()

    for other in range(slabs - 1):

        @pl.when(other < slab)
        def _():
            pl.semaphore_signal(
                ready, inc=1, device_id=(other * SLAB + place, rank), device_id_type=MESH
            )

    for pair in range(pairs // 2, pairs):
        pair_loads(0, pair)
        pair_loads(1, pair)
        later_chunks(pair)
    for head in range(heads):
        for chunk in range(1, chunks):
            product(head, chunk)

    @pl.when(ctx == 0)
    def _():
        halo[...] = jnp.zeros_like(halo)

    @pl.when(ctx > 0)
    def _():
        halo_copy.wait_recv()

    for group in range(groups):
        for pair in range(group * GROUP // 2, (group + 1) * GROUP // 2):
            first_chunk(pair)
        for member in range(GROUP):
            product(group * GROUP + member, 0)
            finish_state(group * GROUP + member, group, member)
        send_states(group)

    load_gain.wait()
    for head in range(heads):
        load(2, head).wait()
        load(3, head).wait()

    def query_part(first, last):
        for head in range(first, last):
            queries(head)
            inner(head)
            gate(head)

    query_part(0, heads - 2)
    for group in range(groups):
        sum_slab(group)
    query_part(heads - 2, heads)
    for group in range(groups):
        send_prefixes(group)

    eye = (
        lax.broadcasted_iota(jnp.int32, (128, 128), 0)
        == lax.broadcasted_iota(jnp.int32, (128, 128), 1)
    )
    half_tokens = tokens // HALVES

    def square_copy(half, step):
        return pltpu.make_async_remote_copy(
            src_ref=send_square.at[half],
            dst_ref=recv_square.at[half, step - 1],
            send_sem=square_send_sem.at[half],
            recv_sem=square_recv_sem.at[half],
            device_id=(ctx, lax.rem(rank + step, ranks)),
            device_id_type=MESH,
        )

    def outer(group, chunk):
        rows = slice(chunk * CHUNK, (chunk + 1) * CHUNK)
        total = None
        for head in range(group * GROUP, (group + 1) * GROUP):
            here = mixed[head, rows] + jnp.dot(
                cooked[2, head, rows], states[head, chunk], preferred_element_type=jnp.float32
            )
            mixed[head, rows] = here * gates[head, rows]
            total = here * here if total is None else total + here * here
        if group > 0:
            total = total + squares[rows]
        if group < groups - 1:
            squares[rows] = total
            return
        column = jnp.sum(total, axis=1, keepdims=True)
        for part in range(CHUNK // 128):
            index = chunk * (CHUNK // 128) + part
            half, line = index // (half_tokens // 128), index % (half_tokens // 128)
            send_square[half, line : line + 1, :] = jnp.sum(
                jnp.where(eye, column[part * 128 : (part + 1) * 128], 0.0), axis=0, keepdims=True
            )

    def finish(half):
        whole(recv_square.at[half], square_recv_sem.at[half]).wait()
        square = send_square[half]
        for step in range(1, ranks):
            square = square + recv_square[half, step - 1]
        factor = lax.rsqrt(square / (channels * ranks) + 1e-06)
        for line in range(half_tokens // 128):
            column = jnp.sum(jnp.where(eye, factor[line : line + 1], 0.0), axis=1, keepdims=True)
            spread = jnp.broadcast_to(column, (128, DH))
            first = half * half_tokens + line * 128
            for head in range(heads):
                out_ref[first : first + 128, lanes(head)] = (
                    mixed[head, first : first + 128] * spread
                ).astype(jnp.bfloat16)

    send_square[...] = jnp.zeros_like(send_square)

    for group in range(groups):
        whole(recv_slices.at[group], prefix_recv_sem.at[group]).wait()
        for member in range(GROUP):
            head = group * GROUP + member
            carried = prefix[group, :, member].reshape(DH, DH).astype(jnp.float32)
            for chunk in range(chunks):
                states[head, chunk] = (carried + part_state[head, chunk]).astype(jnp.bfloat16)
        for chunk in range(chunks):
            outer(group, chunk)
            if group == groups - 1 and (chunk + 1) * CHUNK % half_tokens == 0:
                half = (chunk + 1) * CHUNK // half_tokens - 1
                for step in range(1, ranks):
                    square_copy(half, step).start()
    for half in range(HALVES):
        finish(half)

    for half in range(HALVES):
        whole(recv_square.at[half], square_send_sem.at[half]).wait()
    for group in range(groups):
        whole(recv_slices.at[group], slice_send_sem.at[group]).wait()
        whole(recv_slices.at[group], prefix_send_sem.at[group]).wait()
        for other in range(1, slabs):

            @pl.when(other > slab)
            def _():
                total_copy(group, other).wait_send()

    @pl.when(ctx < ctx_count - 1)
    def _():
        halo_copy.wait_send()


def body(query_raw, key_raw, value_raw, gate_raw, conv_weight, norm_gain):
    tokens, channels = query_raw.shape
    heads = channels // DH
    chunks = tokens // CHUNK
    groups = heads // GROUP
    slabs = lax.axis_size("ctx") // SLAB
    ranks = lax.axis_size("head")
    dma = pltpu.SemaphoreType.DMA
    return pl.pallas_call(
        functools.partial(kernel, (heads, tokens, slabs, ranks)),
        out_shape=pltpu.VMEM((tokens, channels), jnp.bfloat16),
        in_specs=[pl.BlockSpec(memory_space=pltpu.HBM)] * 6,
        out_specs=pl.BlockSpec(memory_space=pltpu.VMEM),
        scratch_shapes=[
            pltpu.VMEM((4, heads, tokens, DH), jnp.bfloat16),
            pltpu.VMEM((3, KW, channels), jnp.float32),
            pltpu.VMEM((heads, DH), jnp.float32),
            pltpu.VMEM((3, heads, tokens, DH), jnp.bfloat16),
            pltpu.VMEM((3, TILE, channels), jnp.bfloat16),
            pltpu.VMEM((TILE, channels), jnp.bfloat16),
            pltpu.VMEM((TILE, channels), jnp.bfloat16),
            pltpu.VMEM((CHUNK, CHUNK), jnp.bfloat16),
            pltpu.VMEM((CHUNK, CHUNK), jnp.bfloat16),
            pltpu.VMEM((heads, tokens, DH), jnp.float32),
            pltpu.VMEM((heads, tokens, DH), jnp.float32),
            pltpu.VMEM((heads, chunks, DH, DH), jnp.float32),
            pltpu.VMEM((heads, chunks, DH, DH), jnp.bfloat16),
            pltpu.VMEM((tokens, DH), jnp.float32),
            pltpu.VMEM((groups, SLAB, GROUP, TILE, DH), jnp.bfloat16),
            pltpu.VMEM((groups, SLAB - 1, GROUP, TILE, DH), jnp.bfloat16),
            pltpu.VMEM((groups, SLAB, GROUP, TILE, DH), jnp.float32),
            pltpu.VMEM((groups, GROUP, TILE, DH), jnp.bfloat16),
            pltpu.VMEM((groups, slabs, GROUP, TILE, DH), jnp.bfloat16),
            pltpu.VMEM((groups, SLAB, GROUP, TILE, DH), jnp.bfloat16),
            pltpu.VMEM((groups, SLAB, GROUP, TILE, DH), jnp.bfloat16),
            pltpu.VMEM((HALVES, 8, 128), jnp.float32),
            pltpu.VMEM((HALVES, ranks - 1, 8, 128), jnp.float32),
            dma((4, heads)),
            dma((2,)),
            dma((3,)),
            dma,
            dma,
            dma((groups,)),
            dma((groups,)),
            dma((groups, slabs)),
            dma((groups, slabs)),
            dma((groups,)),
            dma((groups,)),
            dma((HALVES,)),
            dma((HALVES,)),
            pltpu.SemaphoreType.REGULAR,
        ],
        compiler_params=pltpu.CompilerParams(
            collective_id=0, has_side_effects=True, vmem_limit_bytes=48 * 2**20
        ),
    )(
        *(
            pltpu.with_memory_space_constraint(item, pltpu.HBM)
            for item in (
                query_raw,
                key_raw,
                value_raw,
                gate_raw,
                conv_weight,
                norm_gain.reshape(heads, DH),
            )
        )
    )


def solution(mesh):
    placed = (
        P("ctx", "head"),
        P("ctx", "head"),
        P("ctx", "head"),
        P("ctx", "head"),
        P(None, None, "head"),
        P("head"),
    )
    return jax.shard_map(
        body, mesh=mesh, in_specs=placed, out_specs=P("ctx", "head"), check_vma=False
    )
```

```python
import functools

import jax
import jax.numpy as jnp
from jax import lax
from jax.experimental import pallas as pl
from jax.experimental.pallas import tpu as pltpu
from jax.sharding import PartitionSpec as P

DH = 128
KW = 4
CHUNK = 256
STRIP = 64
TILE = 16
SLAB = 16
GROUP = 4
UNITS = GROUP * (DH // TILE) // SLAB
SUBLANES = 8
STRIDE = CHUNK // SUBLANES
HALVES = 2
MESH = pl.DeviceIdType.MESH
FAR_FIRST = sorted(range(1, SLAB), key=lambda step: (-min(step % 8, 8 - step % 8), -step))


def conv_rows(extended, taps):
    behind = pltpu.roll(extended, 1, 0)
    near = taps[3] * extended + taps[2] * behind
    far = taps[1] * extended + taps[0] * behind
    return (near + pltpu.roll(far, 2, 0))[8:]


def kernel(
    sizes,
    q_hbm,
    k_hbm,
    v_hbm,
    g_hbm,
    taps_hbm,
    gain_hbm,
    out_ref,
    raw,
    taps_ref,
    gain_ref,
    cooked,
    tails,
    tail_pack,
    halo,
    stride_order,
    causal,
    mixed,
    gates,
    part_state,
    states,
    squares,
    send_slices,
    recv_slices,
    before,
    send_total,
    recv_total,
    send_prefix,
    prefix,
    send_square,
    recv_square,
    load_sem,
    small_sem,
    tail_sem,
    halo_send_sem,
    halo_recv_sem,
    slice_send_sem,
    slice_recv_sem,
    total_send_sem,
    total_recv_sem,
    prefix_send_sem,
    prefix_recv_sem,
    square_send_sem,
    square_recv_sem,
    ready,
):
    heads, tokens, slabs, ranks = sizes
    channels = heads * DH
    chunks = tokens // CHUNK
    groups = heads // GROUP
    ctx = lax.axis_index("ctx")
    rank = lax.axis_index("head")
    slab = ctx // SLAB
    place = lax.rem(ctx, SLAB)
    ctx_count = slabs * SLAB

    sources = (k_hbm, v_hbm, q_hbm, g_hbm)

    def load(array, head):
        return pltpu.make_async_copy(
            sources[array].at[:, pl.ds(pl.multiple_of(head * DH, DH), DH)],
            raw.at[array, head],
            load_sem.at[array, head],
        )

    barrier = pltpu.get_barrier_semaphore()

    def greet(target_ctx, target_rank):
        pl.semaphore_signal(
            barrier, inc=1, device_id=(target_ctx, target_rank), device_id_type=MESH
        )

    def load_tail(array):
        return pltpu.make_async_copy(
            sources[array].at[pl.ds(tokens - TILE, TILE), :], tails.at[array], tail_sem.at[array]
        )

    load_taps = pltpu.make_async_copy(taps_hbm, taps_ref, small_sem.at[0])
    load_gain = pltpu.make_async_copy(gain_hbm, gain_ref, small_sem.at[1])
    def start_pair(first, pair):
        for head in (2 * pair, 2 * pair + 1):
            load(first, head).start()
            load(first + 1, head).start()

    load_taps.start()
    start_pair(0, 0)
    start_pair(0, 1)
    for array in range(3):
        load_tail(array).start()

    for step in range(1, SLAB):
        greet(slab * SLAB + lax.rem(place + step, SLAB), rank)
    for step in range(1, ranks):
        greet(ctx, lax.rem(rank + step, ranks))

    @pl.when(ctx > 0)
    def _():
        greet(ctx - 1, rank)

    @pl.when(ctx < ctx_count - 1)
    def _():
        greet(ctx + 1, rank)

    for other in range(1, slabs):

        @pl.when(other > slab)
        def _():
            greet(other * SLAB + place, rank)

    row = lax.broadcasted_iota(jnp.int32, (CHUNK, CHUNK), 0)
    column = lax.broadcasted_iota(jnp.int32, (CHUNK, CHUNK), 1)

    def token_of(position):
        return position % SUBLANES * STRIDE + position // SUBLANES

    stride_order[...] = jnp.where(column == token_of(row), 1.0, 0.0).astype(jnp.bfloat16)
    causal[...] = jnp.where(row >= token_of(column), 1.0, 0.0).astype(jnp.bfloat16)

    halo_copy = pltpu.make_async_remote_copy(
        src_ref=tail_pack,
        dst_ref=halo,
        send_sem=halo_send_sem,
        recv_sem=halo_recv_sem,
        device_id=(ctx + 1, rank),
        device_id_type=MESH,
    )

    def lanes(head):
        return slice(head * DH, (head + 1) * DH)

    def taps_of(kind, head, factor):
        return [taps_ref[kind, j : j + 1, lanes(head)] * factor for j in range(KW)]

    first_sublane = lax.broadcasted_iota(jnp.int32, (SUBLANES, DH), 0) == 0

    def conv_strided(rows, ahead, taps):
        edge = [
            jnp.where(
                first_sublane,
                ahead[j],
                pltpu.roll(rows[CHUNK + (j - 3) * SUBLANES :][:SUBLANES], 1, 0),
            )
            for j in range(KW - 1)
        ]
        extended = jnp.concatenate(edge + [rows], axis=0)
        terms = [
            taps[j] * extended[j * SUBLANES : j * SUBLANES + CHUNK] for j in range(KW)
        ]
        return (terms[3] + terms[2]) + (terms[1] + terms[0])

    def last_rows(rows):
        return [
            pltpu.roll(rows[CHUNK + (j - 3) * SUBLANES :][:SUBLANES], 1, 0) for j in range(KW - 1)
        ]

    def in_stride_order(array, pair, chunk):
        rows = slice(chunk * CHUNK, (chunk + 1) * CHUNK)
        both = jnp.concatenate([raw[array, 2 * pair, rows], raw[array, 2 * pair + 1, rows]], axis=1)
        return jnp.dot(stride_order[...], both, preferred_element_type=jnp.float32)

    def keys_values(pair, chunk, rows_of, ahead_of):
        for member in range(2):
            head = 2 * pair + member
            here = slice(member * DH, (member + 1) * DH)
            rows = slice(chunk * CHUNK, (chunk + 1) * CHUNK)
            half = conv_strided(rows_of[0][:, here], ahead_of(0, member), taps_of(1, head, 0.5))
            cooked[0, head, rows] = (half + half * jnp.tanh(half)).astype(jnp.bfloat16)
            cooked[1, head, rows] = conv_strided(
                rows_of[1][:, here], ahead_of(1, member), taps_of(2, head, 1.0)
            ).astype(jnp.bfloat16)

    def later_chunks(pair):
        previous = [in_stride_order(array, pair, 0) for array in range(2)]
        for chunk in range(1, chunks):
            behind = [last_rows(item) for item in previous]

            def ahead_of(array, member):
                return [item[:, member * DH : (member + 1) * DH] for item in behind[array]]

            previous = [in_stride_order(array, pair, chunk) for array in range(2)]
            keys_values(pair, chunk, previous, ahead_of)

    def first_chunk(pair):
        def ahead_of(array, member):
            head = 2 * pair + member
            rows = halo[:, lanes(head)].astype(jnp.float32)
            return [rows[array * 3 + j : array * 3 + j + 1] for j in range(KW - 1)]

        keys_values(pair, 0, [in_stride_order(array, pair, 0) for array in range(2)], ahead_of)

    def product(head, chunk):
        rows = slice(chunk * CHUNK, (chunk + 1) * CHUNK)
        part_state[head, chunk] = lax.dot_general(
            cooked[0, head, rows],
            cooked[1, head, rows],
            (((0,), (0,)), ((), ())),
            preferred_element_type=jnp.float32,
        )

    def pack_tails():
        wide = lax.broadcasted_iota(jnp.int32, (TILE, channels), 0)
        key, value, query = [
            pltpu.roll(tails[array].astype(jnp.float32), 3 * (array + 1), 0) for array in range(3)
        ]
        packed = jnp.where(wide < 3, key, jnp.where(wide < 6, value, query))
        tail_pack[...] = packed.astype(jnp.bfloat16)

    def extended_rows(array, head, row):
        if row == 0:
            ahead = halo[:, lanes(head)].astype(jnp.float32)
            own = raw[array, head, 0:STRIP, :]
            return jnp.concatenate(
                [pltpu.roll(ahead, TILE - 1, 0)[:SUBLANES], own.astype(jnp.float32)], axis=0
            )
        return raw[array, head, row - TILE : row + STRIP, :].astype(jnp.float32)[8:]

    def finish_state(head, group, member):
        running = part_state[head, 0]
        for chunk in range(1, chunks):
            own = part_state[head, chunk]
            part_state[head, chunk] = running
            running = running + own
        part_state[head, 0] = jnp.zeros((DH, DH), jnp.float32)
        rounded = running.astype(jnp.bfloat16)
        for piece in range(DH // TILE):
            owner = member // UNITS * (DH // TILE) + piece
            send_slices[group, owner, member % UNITS] = rounded[piece * TILE : (piece + 1) * TILE]

    def peer(step):
        return lax.rem(place + step, SLAB)

    def slice_copy(group, step):
        return pltpu.make_async_remote_copy(
            src_ref=send_slices.at[group, peer(step)],
            dst_ref=recv_slices.at[group, step - 1],
            send_sem=slice_send_sem.at[group],
            recv_sem=slice_recv_sem.at[group],
            device_id=(slab * SLAB + peer(step), rank),
            device_id_type=MESH,
        )

    def total_copy(group, other):
        return pltpu.make_async_remote_copy(
            src_ref=send_total.at[group],
            dst_ref=recv_total.at[group, slab],
            send_sem=total_send_sem.at[group, other],
            recv_sem=total_recv_sem.at[group, slab],
            device_id=(other * SLAB + place, rank),
            device_id_type=MESH,
        )

    def total_arrival(group, other):
        return pltpu.make_async_remote_copy(
            src_ref=send_total.at[group],
            dst_ref=recv_total.at[group, other],
            send_sem=total_send_sem.at[group, other],
            recv_sem=total_recv_sem.at[group, other],
            device_id=(other * SLAB + place, rank),
            device_id_type=MESH,
        )

    def prefix_copy(group, step):
        return pltpu.make_async_remote_copy(
            src_ref=send_prefix.at[group, peer(step)],
            dst_ref=prefix.at[group, place],
            send_sem=prefix_send_sem.at[group],
            recv_sem=prefix_recv_sem.at[group],
            device_id=(slab * SLAB + peer(step), rank),
            device_id_type=MESH,
        )

    def whole(ref, sem):
        return pltpu.make_async_copy(ref, ref, sem)

    def send_states(group):
        for step in FAR_FIRST:
            slice_copy(group, step).start()

    def sum_slab(group):
        whole(recv_slices.at[group], slice_recv_sem.at[group]).wait()
        total = send_slices[group, place].astype(jnp.float32)
        for step in range(1, SLAB):
            total = total + recv_slices[group, step - 1].astype(jnp.float32)
        send_total[group] = total.astype(jnp.bfloat16)
        if group == 0:

            @pl.when(slab < slabs - 1)
            def _():
                pl.semaphore_wait(ready, slabs - 1 - slab)

        for other in range(slabs - 1, 0, -1):

            @pl.when(other > slab)
            def _():
                total_copy(group, other).start()

    def sum_before(group):
        running = jnp.zeros((UNITS, TILE, DH), jnp.float32)
        for index in range(SLAB):
            before[group, index] = running
            if index < SLAB - 1:
                step = lax.rem(place - index + SLAB, SLAB)
                got = recv_slices[group, jnp.maximum(step - 1, 0)].astype(jnp.float32)
                own = send_slices[group, place].astype(jnp.float32)
                running = running + jnp.where(step == 0, own, got)

    def send_prefixes(group):
        def add(other, total):
            total_arrival(group, other).wait_recv()
            return total + recv_total[group, other].astype(jnp.float32)

        earlier = lax.fori_loop(0, slab, add, jnp.zeros((UNITS, TILE, DH), jnp.float32))
        for index in range(SLAB):
            send_prefix[group, index] = (earlier + before[group, index]).astype(jnp.bfloat16)
        for step in FAR_FIRST:
            prefix_copy(group, step).start()
        prefix[group, place] = send_prefix[group, place]

    def queries(head):
        query_taps = taps_of(0, head, 0.5)
        for row in range(0, tokens, STRIP):
            half = conv_rows(extended_rows(2, head, row), query_taps)
            scaled = half * DH ** (-0.5)
            cooked[2, head, row : row + STRIP, :] = (scaled + scaled * jnp.tanh(half)).astype(
                jnp.bfloat16
            )

    def inner(head):
        for chunk in range(chunks):
            rows = slice(chunk * CHUNK, (chunk + 1) * CHUNK)
            scores = lax.dot_general(
                cooked[2, head, rows],
                cooked[0, head, rows],
                (((1,), (1,)), ((), ())),
                preferred_element_type=jnp.float32,
            )
            weights = scores.astype(jnp.bfloat16) * causal[...]
            mixed[head, rows] = jnp.dot(
                weights, cooked[1, head, rows], preferred_element_type=jnp.float32
            )

    def gate(head):
        gain = gain_ref[pl.ds(head, 1), :] * 0.5
        for row in range(0, tokens, STRIP):
            half = raw[3, head, row : row + STRIP, :].astype(jnp.float32) * 0.5
            gates[head, row : row + STRIP, :] = gain + gain * jnp.tanh(half)

    pairs = heads // 2

    def pair_loads(array, pair):
        load(array, 2 * pair).wait()
        load(array, 2 * pair + 1).wait()

    load_taps.wait()
    for pair in range(pairs // 2):
        pair_loads(0, pair)
        pair_loads(1, pair)
        start_pair(0, pair + 2)
        later_chunks(pair)

    for array in range(3):
        load_tail(array).wait()
    pack_tails()
    pl.semaphore_wait(
        barrier,
        SLAB - 1 + ranks - 1 + slab + jnp.minimum(ctx, 1) + jnp.minimum(ctx_count - 1 - ctx, 1),
    )

    @pl.when(ctx < ctx_count - 1)
    def _():
        halo_copy.start()

    for other in range(slabs - 1):

        @pl.when(other < slab)
        def _():
            pl.semaphore_signal(
                ready, inc=1, device_id=(other * SLAB + place, rank), device_id_type=MESH
            )

    load_gain.start()
    for pair in range(pairs // 2, pairs):
        pair_loads(0, pair)
        pair_loads(1, pair)
        start_pair(2, 2 * pair - pairs)
        start_pair(2, 2 * pair - pairs + 1)
        later_chunks(pair)
    for head in range(heads):
        for chunk in range(1, chunks):
            product(head, chunk)

    @pl.when(ctx == 0)
    def _():
        halo[...] = jnp.zeros_like(halo)

    @pl.when(ctx > 0)
    def _():
        halo_copy.wait_recv()

    for group in range(groups):
        for pair in range(group * GROUP // 2, (group + 1) * GROUP // 2):
            first_chunk(pair)
        for member in range(GROUP):
            product(group * GROUP + member, 0)
            finish_state(group * GROUP + member, group, member)
        send_states(group)

    load_gain.wait()
    for head in range(heads):
        load(2, head).wait()
        load(3, head).wait()

    def query_part(first, last):
        for head in range(first, last):
            queries(head)
            inner(head)
            gate(head)

    query_part(0, heads - 2)
    for group in range(groups):
        sum_slab(group)
    for group in range(groups):
        sum_before(group)
    query_part(heads - 2, heads)
    states[...] = jnp.zeros_like(states)
    send_square[...] = jnp.zeros_like(send_square)
    for group in range(groups):
        send_prefixes(group)

    eye = (
        lax.broadcasted_iota(jnp.int32, (128, 128), 0)
        == lax.broadcasted_iota(jnp.int32, (128, 128), 1)
    )
    half_tokens = tokens // HALVES

    def square_copy(half, step):
        return pltpu.make_async_remote_copy(
            src_ref=send_square.at[half],
            dst_ref=recv_square.at[half, step - 1],
            send_sem=square_send_sem.at[half],
            recv_sem=square_recv_sem.at[half],
            device_id=(ctx, lax.rem(rank + step, ranks)),
            device_id_type=MESH,
        )

    def outer(group, chunk):
        rows = slice(chunk * CHUNK, (chunk + 1) * CHUNK)
        total = None
        for pair in range(group * GROUP // 2, (group + 1) * GROUP // 2):
            both = jnp.concatenate(
                [cooked[2, 2 * pair, rows], cooked[2, 2 * pair + 1, rows]], axis=1
            )
            carried = jnp.dot(both, states[pair, chunk], preferred_element_type=jnp.float32)
            for member in range(2):
                head = 2 * pair + member
                here = mixed[head, rows] + carried[:, member * DH : (member + 1) * DH]
                mixed[head, rows] = here * gates[head, rows]
                total = here * here if total is None else total + here * here
        if group > 0:
            total = total + squares[rows]
        if group < groups - 1:
            squares[rows] = total
            return
        column = jnp.sum(total, axis=1, keepdims=True)
        for part in range(CHUNK // 128):
            index = chunk * (CHUNK // 128) + part
            half, line = index // (half_tokens // 128), index % (half_tokens // 128)
            send_square[half, line : line + 1, :] = jnp.sum(
                jnp.where(eye, column[part * 128 : (part + 1) * 128], 0.0), axis=0, keepdims=True
            )

    def finish(half):
        whole(recv_square.at[half], square_recv_sem.at[half]).wait()
        square = send_square[half]
        for step in range(1, ranks):
            square = square + recv_square[half, step - 1]
        factor = lax.rsqrt(square / (channels * ranks) + 1e-06)
        for line in range(half_tokens // 128):
            column = jnp.sum(jnp.where(eye, factor[line : line + 1], 0.0), axis=1, keepdims=True)
            spread = jnp.broadcast_to(column, (128, DH))
            first = half * half_tokens + line * 128
            for head in range(heads):
                out_ref[first : first + 128, lanes(head)] = (
                    mixed[head, first : first + 128] * spread
                ).astype(jnp.bfloat16)

    for group in range(groups):
        whole(recv_slices.at[group], prefix_recv_sem.at[group]).wait()
        for member in range(GROUP):
            head = group * GROUP + member
            first = member // UNITS * (DH // TILE)
            carried = prefix[group, first : first + DH // TILE, member % UNITS]
            carried = carried.reshape(DH, DH).astype(jnp.float32)
            for chunk in range(chunks):
                block = slice(head % 2 * DH, (head % 2 + 1) * DH)
                states[head // 2, chunk, block, block] = (
                    carried + part_state[head, chunk]
                ).astype(jnp.bfloat16)
        for chunk in range(chunks):
            outer(group, chunk)
            if group == groups - 1 and (chunk + 1) * CHUNK % half_tokens == 0:
                half = (chunk + 1) * CHUNK // half_tokens - 1
                for step in range(1, ranks):
                    square_copy(half, step).start()
    for half in range(HALVES):
        finish(half)

    for half in range(HALVES):
        whole(recv_square.at[half], square_send_sem.at[half]).wait()
    for group in range(groups):
        whole(recv_slices.at[group], slice_send_sem.at[group]).wait()
        whole(recv_slices.at[group], prefix_send_sem.at[group]).wait()
        for other in range(1, slabs):

            @pl.when(other > slab)
            def _():
                total_copy(group, other).wait_send()

    @pl.when(ctx < ctx_count - 1)
    def _():
        halo_copy.wait_send()


def body(query_raw, key_raw, value_raw, gate_raw, conv_weight, norm_gain):
    tokens, channels = query_raw.shape
    heads = channels // DH
    chunks = tokens // CHUNK
    groups = heads // GROUP
    slabs = lax.axis_size("ctx") // SLAB
    ranks = lax.axis_size("head")
    dma = pltpu.SemaphoreType.DMA
    return pl.pallas_call(
        functools.partial(kernel, (heads, tokens, slabs, ranks)),
        out_shape=pltpu.VMEM((tokens, channels), jnp.bfloat16),
        in_specs=[pl.BlockSpec(memory_space=pltpu.HBM)] * 6,
        out_specs=pl.BlockSpec(memory_space=pltpu.VMEM),
        scratch_shapes=[
            pltpu.VMEM((4, heads, tokens, DH), jnp.bfloat16),
            pltpu.VMEM((3, KW, channels), jnp.float32),
            pltpu.VMEM((heads, DH), jnp.float32),
            pltpu.VMEM((3, heads, tokens, DH), jnp.bfloat16),
            pltpu.VMEM((3, TILE, channels), jnp.bfloat16),
            pltpu.VMEM((TILE, channels), jnp.bfloat16),
            pltpu.VMEM((TILE, channels), jnp.bfloat16),
            pltpu.VMEM((CHUNK, CHUNK), jnp.bfloat16),
            pltpu.VMEM((CHUNK, CHUNK), jnp.bfloat16),
            pltpu.VMEM((heads, tokens, DH), jnp.float32),
            pltpu.VMEM((heads, tokens, DH), jnp.float32),
            pltpu.VMEM((heads, chunks, DH, DH), jnp.float32),
            pltpu.VMEM((heads // 2, chunks, 2 * DH, 2 * DH), jnp.bfloat16),
            pltpu.VMEM((tokens, DH), jnp.float32),
            pltpu.VMEM((groups, SLAB, UNITS, TILE, DH), jnp.bfloat16),
            pltpu.VMEM((groups, SLAB - 1, UNITS, TILE, DH), jnp.bfloat16),
            pltpu.VMEM((groups, SLAB, UNITS, TILE, DH), jnp.float32),
            pltpu.VMEM((groups, UNITS, TILE, DH), jnp.bfloat16),
            pltpu.VMEM((groups, slabs, UNITS, TILE, DH), jnp.bfloat16),
            pltpu.VMEM((groups, SLAB, UNITS, TILE, DH), jnp.bfloat16),
            pltpu.VMEM((groups, SLAB, UNITS, TILE, DH), jnp.bfloat16),
            pltpu.VMEM((HALVES, 8, 128), jnp.float32),
            pltpu.VMEM((HALVES, ranks - 1, 8, 128), jnp.float32),
            dma((4, heads)),
            dma((2,)),
            dma((3,)),
            dma,
            dma,
            dma((groups,)),
            dma((groups,)),
            dma((groups, slabs)),
            dma((groups, slabs)),
            dma((groups,)),
            dma((groups,)),
            dma((HALVES,)),
            dma((HALVES,)),
            pltpu.SemaphoreType.REGULAR,
        ],
        compiler_params=pltpu.CompilerParams(
            collective_id=0, has_side_effects=True, vmem_limit_bytes=48 * 2**20
        ),
    )(
        *(
            pltpu.with_memory_space_constraint(item, pltpu.HBM)
            for item in (
                query_raw,
                key_raw,
                value_raw,
                gate_raw,
                conv_weight,
                norm_gain.reshape(heads, DH),
            )
        )
    )


def solution(mesh):
    placed = (
        P("ctx", "head"),
        P("ctx", "head"),
        P("ctx", "head"),
        P("ctx", "head"),
        P(None, None, "head"),
        P("head"),
    )
    return jax.shard_map(
        body, mesh=mesh, in_specs=placed, out_specs=P("ctx", "head"), check_vma=False
    )
```

```python
import functools

import jax
import jax.numpy as jnp
from jax import lax
from jax.experimental import pallas as pl
from jax.experimental.pallas import tpu as pltpu
from jax.sharding import PartitionSpec as P

DH = 128
KW = 4
CHUNK = 256
STRIP = 64
TILE = 16
SLAB = 16
GROUP = 4
UNITS = GROUP * (DH // TILE) // SLAB
SUBLANES = 8
STRIDE = CHUNK // SUBLANES
RIM = 32
HALVES = 2
MESH = pl.DeviceIdType.MESH
FAR_FIRST = sorted(range(1, SLAB), key=lambda step: (-min(step % 8, 8 - step % 8), -step))


def conv_rows(extended, taps):
    behind = pltpu.roll(extended, 1, 0)
    near = taps[3] * extended + taps[2] * behind
    far = taps[1] * extended + taps[0] * behind
    return (near + pltpu.roll(far, 2, 0))[8:]


def kernel(
    sizes,
    q_hbm,
    k_hbm,
    v_hbm,
    g_hbm,
    taps_hbm,
    gain_hbm,
    out_ref,
    raw,
    taps_ref,
    gain_ref,
    cooked,
    tails,
    tail_pack,
    halo,
    rim,
    later_state,
    stride_order,
    causal,
    mixed,
    gates,
    part_state,
    states,
    squares,
    send_slices,
    recv_slices,
    before,
    send_total,
    recv_total,
    send_prefix,
    prefix,
    send_square,
    recv_square,
    load_sem,
    small_sem,
    tail_sem,
    halo_send_sem,
    halo_recv_sem,
    slice_send_sem,
    slice_recv_sem,
    total_send_sem,
    total_recv_sem,
    prefix_send_sem,
    prefix_recv_sem,
    square_send_sem,
    square_recv_sem,
    ready,
):
    heads, tokens, slabs, ranks = sizes
    channels = heads * DH
    chunks = tokens // CHUNK
    groups = heads // GROUP
    ctx = lax.axis_index("ctx")
    rank = lax.axis_index("head")
    slab = ctx // SLAB
    place = lax.rem(ctx, SLAB)
    ctx_count = slabs * SLAB

    sources = (k_hbm, v_hbm, q_hbm, g_hbm)

    def load(array, head):
        return pltpu.make_async_copy(
            sources[array].at[:, pl.ds(pl.multiple_of(head * DH, DH), DH)],
            raw.at[array, head],
            load_sem.at[array, head],
        )

    barrier = pltpu.get_barrier_semaphore()

    def greet(target_ctx, target_rank):
        pl.semaphore_signal(
            barrier, inc=1, device_id=(target_ctx, target_rank), device_id_type=MESH
        )

    def load_tail(array):
        return pltpu.make_async_copy(
            sources[array].at[pl.ds(tokens - TILE, TILE), :], tails.at[array], tail_sem.at[array]
        )

    load_taps = pltpu.make_async_copy(taps_hbm, taps_ref, small_sem.at[0])
    load_gain = pltpu.make_async_copy(gain_hbm, gain_ref, small_sem.at[1])
    def start_pair(first, pair):
        for head in (2 * pair, 2 * pair + 1):
            load(first, head).start()
            load(first + 1, head).start()

    load_taps.start()
    start_pair(0, 0)
    start_pair(0, 1)
    for array in range(3):
        load_tail(array).start()

    for step in range(1, SLAB):
        greet(slab * SLAB + lax.rem(place + step, SLAB), rank)
    for step in range(1, ranks):
        greet(ctx, lax.rem(rank + step, ranks))

    @pl.when(ctx > 0)
    def _():
        greet(ctx - 1, rank)

    @pl.when(ctx < ctx_count - 1)
    def _():
        greet(ctx + 1, rank)

    for other in range(1, slabs):

        @pl.when(other > slab)
        def _():
            greet(other * SLAB + place, rank)

    row = lax.broadcasted_iota(jnp.int32, (CHUNK, CHUNK), 0)
    column = lax.broadcasted_iota(jnp.int32, (CHUNK, CHUNK), 1)

    def token_of(position):
        return position % SUBLANES * STRIDE + position // SUBLANES

    stride_order[...] = jnp.where(column == token_of(row), 1.0, 0.0).astype(jnp.bfloat16)
    causal[...] = jnp.where(row >= token_of(column), 1.0, 0.0).astype(jnp.bfloat16)

    halo_copy = pltpu.make_async_remote_copy(
        src_ref=tail_pack,
        dst_ref=halo,
        send_sem=halo_send_sem,
        recv_sem=halo_recv_sem,
        device_id=(ctx + 1, rank),
        device_id_type=MESH,
    )

    def lanes(head):
        return slice(head * DH, (head + 1) * DH)

    def taps_of(kind, head, factor):
        return [taps_ref[kind, j : j + 1, lanes(head)] * factor for j in range(KW)]

    first_sublane = lax.broadcasted_iota(jnp.int32, (SUBLANES, DH), 0) == 0

    def last_rows(rows):
        return [
            pltpu.roll(rows[CHUNK + (j - 3) * SUBLANES :][:SUBLANES], 1, 0) for j in range(KW - 1)
        ]

    def conv_strided(extended, taps):
        count = extended.shape[0] - (KW - 1) * SUBLANES
        terms = [taps[j] * extended[j * SUBLANES : j * SUBLANES + count] for j in range(KW)]
        return (terms[3] + terms[2]) + (terms[1] + terms[0])

    def cook(array, head, rows, extended):
        if array == 0:
            half = conv_strided(extended, taps_of(1, head, 0.5))
            cooked[0, head, rows] = (half + half * jnp.tanh(half)).astype(jnp.bfloat16)
        else:
            cooked[1, head, rows] = conv_strided(extended, taps_of(2, head, 1.0)).astype(
                jnp.bfloat16
            )

    def in_stride_order(array, pair, chunk):
        rows = slice(chunk * CHUNK, (chunk + 1) * CHUNK)
        both = jnp.concatenate([raw[array, 2 * pair, rows], raw[array, 2 * pair + 1, rows]], axis=1)
        return jnp.dot(stride_order[...], both, preferred_element_type=jnp.float32)

    def keys_values(pair):
        behind = None
        for chunk in range(chunks):
            rows_of = [in_stride_order(array, pair, chunk) for array in range(2)]
            last = [last_rows(item) for item in rows_of]
            for member in range(2):
                head = 2 * pair + member
                here = slice(member * DH, (member + 1) * DH)
                for array in range(2):
                    rows = rows_of[array][:, here]
                    edge = [item[:, here] for item in last[array]]
                    if chunk == 0:
                        rim[array, head] = jnp.concatenate(edge + [rows[:RIM]], axis=0)
                        cook(
                            array,
                            head,
                            slice(RIM, CHUNK),
                            rows[RIM - (KW - 1) * SUBLANES :],
                        )
                    else:
                        edge = [
                            jnp.where(first_sublane, before_it[:, here], after_it)
                            for before_it, after_it in zip(behind[array], edge)
                        ]
                        cook(
                            array,
                            head,
                            slice(chunk * CHUNK, (chunk + 1) * CHUNK),
                            jnp.concatenate(edge + [rows], axis=0),
                        )
            behind = last

    def finish_rim(head):
        arrived = halo[:, lanes(head)].astype(jnp.float32)
        for array in range(2):
            edge = [
                jnp.where(
                    first_sublane,
                    arrived[array * 3 + j : array * 3 + j + 1],
                    rim[array, head, j * SUBLANES : (j + 1) * SUBLANES],
                )
                for j in range(KW - 1)
            ]
            rows = rim[array, head, (KW - 1) * SUBLANES :]
            cook(array, head, slice(0, RIM), jnp.concatenate(edge + [rows], axis=0))

    def product(head, chunk):
        rows = slice(chunk * CHUNK, (chunk + 1) * CHUNK)
        part_state[head, chunk] = lax.dot_general(
            cooked[0, head, rows],
            cooked[1, head, rows],
            (((0,), (0,)), ((), ())),
            preferred_element_type=jnp.float32,
        )

    def pack_tails():
        wide = lax.broadcasted_iota(jnp.int32, (TILE, channels), 0)
        key, value, query = [
            pltpu.roll(tails[array].astype(jnp.float32), 3 * (array + 1), 0) for array in range(3)
        ]
        packed = jnp.where(wide < 3, key, jnp.where(wide < 6, value, query))
        tail_pack[...] = packed.astype(jnp.bfloat16)

    def extended_rows(array, head, row):
        if row == 0:
            ahead = halo[:, lanes(head)].astype(jnp.float32)
            own = raw[array, head, 0:STRIP, :]
            return jnp.concatenate(
                [pltpu.roll(ahead, TILE - 1, 0)[:SUBLANES], own.astype(jnp.float32)], axis=0
            )
        return raw[array, head, row - TILE : row + STRIP, :].astype(jnp.float32)[8:]

    def sum_later(head):
        total = part_state[head, 1]
        for chunk in range(2, chunks):
            total = total + part_state[head, chunk]
        later_state[head] = total

    def finish_state(head, group, member):
        rounded = (part_state[head, 0] + later_state[head]).astype(jnp.bfloat16)
        for piece in range(DH // TILE):
            owner = member // UNITS * (DH // TILE) + piece
            send_slices[group, owner, member % UNITS] = rounded[piece * TILE : (piece + 1) * TILE]

    def chunk_prefixes(head):
        running = part_state[head, 0]
        for chunk in range(1, chunks):
            own = part_state[head, chunk]
            part_state[head, chunk] = running
            running = running + own
        part_state[head, 0] = jnp.zeros((DH, DH), jnp.float32)

    def peer(step):
        return lax.rem(place + step, SLAB)

    def slice_copy(group, step):
        return pltpu.make_async_remote_copy(
            src_ref=send_slices.at[group, peer(step)],
            dst_ref=recv_slices.at[group, step - 1],
            send_sem=slice_send_sem.at[group],
            recv_sem=slice_recv_sem.at[group],
            device_id=(slab * SLAB + peer(step), rank),
            device_id_type=MESH,
        )

    def total_copy(group, other):
        return pltpu.make_async_remote_copy(
            src_ref=send_total.at[group],
            dst_ref=recv_total.at[group, slab],
            send_sem=total_send_sem.at[group, other],
            recv_sem=total_recv_sem.at[group, slab],
            device_id=(other * SLAB + place, rank),
            device_id_type=MESH,
        )

    def total_arrival(group, other):
        return pltpu.make_async_remote_copy(
            src_ref=send_total.at[group],
            dst_ref=recv_total.at[group, other],
            send_sem=total_send_sem.at[group, other],
            recv_sem=total_recv_sem.at[group, other],
            device_id=(other * SLAB + place, rank),
            device_id_type=MESH,
        )

    def prefix_copy(group, step):
        return pltpu.make_async_remote_copy(
            src_ref=send_prefix.at[group, peer(step)],
            dst_ref=prefix.at[group, place],
            send_sem=prefix_send_sem.at[group],
            recv_sem=prefix_recv_sem.at[group],
            device_id=(slab * SLAB + peer(step), rank),
            device_id_type=MESH,
        )

    def whole(ref, sem):
        return pltpu.make_async_copy(ref, ref, sem)

    def send_states(group):
        for step in FAR_FIRST:
            slice_copy(group, step).start()

    def sum_slab(group):
        whole(recv_slices.at[group], slice_recv_sem.at[group]).wait()
        total = send_slices[group, place].astype(jnp.float32)
        for step in range(1, SLAB):
            total = total + recv_slices[group, step - 1].astype(jnp.float32)
        send_total[group] = total.astype(jnp.bfloat16)
        if group == 0:

            @pl.when(slab < slabs - 1)
            def _():
                pl.semaphore_wait(ready, slabs - 1 - slab)

        for other in range(slabs - 1, 0, -1):

            @pl.when(other > slab)
            def _():
                total_copy(group, other).start()

    def sum_before(group):
        running = jnp.zeros((UNITS, TILE, DH), jnp.float32)
        for index in range(SLAB):
            before[group, index] = running
            if index < SLAB - 1:
                step = lax.rem(place - index + SLAB, SLAB)
                got = recv_slices[group, jnp.maximum(step - 1, 0)].astype(jnp.float32)
                own = send_slices[group, place].astype(jnp.float32)
                running = running + jnp.where(step == 0, own, got)

    def send_prefixes(group):
        def add(other, total):
            total_arrival(group, other).wait_recv()
            return total + recv_total[group, other].astype(jnp.float32)

        earlier = lax.fori_loop(0, slab, add, jnp.zeros((UNITS, TILE, DH), jnp.float32))
        for index in range(SLAB):
            send_prefix[group, index] = (earlier + before[group, index]).astype(jnp.bfloat16)
        for step in FAR_FIRST:
            prefix_copy(group, step).start()
        prefix[group, place] = send_prefix[group, place]

    def queries(head):
        query_taps = taps_of(0, head, 0.5)
        for row in range(0, tokens, STRIP):
            half = conv_rows(extended_rows(2, head, row), query_taps)
            scaled = half * DH ** (-0.5)
            cooked[2, head, row : row + STRIP, :] = (scaled + scaled * jnp.tanh(half)).astype(
                jnp.bfloat16
            )

    def inner(head):
        for chunk in range(chunks):
            rows = slice(chunk * CHUNK, (chunk + 1) * CHUNK)
            scores = lax.dot_general(
                cooked[2, head, rows],
                cooked[0, head, rows],
                (((1,), (1,)), ((), ())),
                preferred_element_type=jnp.float32,
            )
            weights = scores.astype(jnp.bfloat16) * causal[...]
            mixed[head, rows] = jnp.dot(
                weights, cooked[1, head, rows], preferred_element_type=jnp.float32
            )

    def gate(head):
        gain = gain_ref[pl.ds(head, 1), :] * 0.5
        for row in range(0, tokens, STRIP):
            half = raw[3, head, row : row + STRIP, :].astype(jnp.float32) * 0.5
            gates[head, row : row + STRIP, :] = gain + gain * jnp.tanh(half)

    pairs = heads // 2

    def pair_loads(array, pair):
        load(array, 2 * pair).wait()
        load(array, 2 * pair + 1).wait()

    load_taps.wait()
    for pair in range(pairs // 2):
        pair_loads(0, pair)
        pair_loads(1, pair)
        start_pair(0, pair + 2)
        keys_values(pair)

    for array in range(3):
        load_tail(array).wait()
    pack_tails()
    pl.semaphore_wait(
        barrier,
        SLAB - 1 + ranks - 1 + slab + jnp.minimum(ctx, 1) + jnp.minimum(ctx_count - 1 - ctx, 1),
    )

    @pl.when(ctx < ctx_count - 1)
    def _():
        halo_copy.start()

    for other in range(slabs - 1):

        @pl.when(other < slab)
        def _():
            pl.semaphore_signal(
                ready, inc=1, device_id=(other * SLAB + place, rank), device_id_type=MESH
            )

    load_gain.start()
    for pair in range(pairs // 2, pairs):
        pair_loads(0, pair)
        pair_loads(1, pair)
        start_pair(2, 2 * pair - pairs)
        start_pair(2, 2 * pair - pairs + 1)
        keys_values(pair)
    for head in range(heads):
        for chunk in range(1, chunks):
            product(head, chunk)
        sum_later(head)

    @pl.when(ctx == 0)
    def _():
        halo[...] = jnp.zeros_like(halo)

    @pl.when(ctx > 0)
    def _():
        halo_copy.wait_recv()

    for group in range(groups):
        for member in range(GROUP):
            finish_rim(group * GROUP + member)
        for member in range(GROUP):
            product(group * GROUP + member, 0)
            finish_state(group * GROUP + member, group, member)
        send_states(group)

    load_gain.wait()
    for head in range(heads):
        chunk_prefixes(head)
    for head in range(heads):
        load(2, head).wait()
        load(3, head).wait()

    def query_part(first, last):
        for head in range(first, last):
            queries(head)
            inner(head)
            gate(head)

    query_part(0, heads - 2)
    for group in range(groups):
        sum_slab(group)
    for group in range(groups):
        sum_before(group)
    query_part(heads - 2, heads)
    states[...] = jnp.zeros_like(states)
    send_square[...] = jnp.zeros_like(send_square)
    for group in range(groups):
        send_prefixes(group)

    eye = (
        lax.broadcasted_iota(jnp.int32, (128, 128), 0)
        == lax.broadcasted_iota(jnp.int32, (128, 128), 1)
    )
    half_tokens = tokens // HALVES

    def square_copy(half, step):
        return pltpu.make_async_remote_copy(
            src_ref=send_square.at[half],
            dst_ref=recv_square.at[half, step - 1],
            send_sem=square_send_sem.at[half],
            recv_sem=square_recv_sem.at[half],
            device_id=(ctx, lax.rem(rank + step, ranks)),
            device_id_type=MESH,
        )

    def outer(group, chunk):
        rows = slice(chunk * CHUNK, (chunk + 1) * CHUNK)
        total = None
        for pair in range(group * GROUP // 2, (group + 1) * GROUP // 2):
            both = jnp.concatenate(
                [cooked[2, 2 * pair, rows], cooked[2, 2 * pair + 1, rows]], axis=1
            )
            carried = jnp.dot(both, states[pair, chunk], preferred_element_type=jnp.float32)
            for member in range(2):
                head = 2 * pair + member
                here = mixed[head, rows] + carried[:, member * DH : (member + 1) * DH]
                mixed[head, rows] = here * gates[head, rows]
                total = here * here if total is None else total + here * here
        if group > 0:
            total = total + squares[rows]
        if group < groups - 1:
            squares[rows] = total
            return
        column = jnp.sum(total, axis=1, keepdims=True)
        for part in range(CHUNK // 128):
            index = chunk * (CHUNK // 128) + part
            half, line = index // (half_tokens // 128), index % (half_tokens // 128)
            send_square[half, line : line + 1, :] = jnp.sum(
                jnp.where(eye, column[part * 128 : (part + 1) * 128], 0.0), axis=0, keepdims=True
            )

    def finish(half):
        whole(recv_square.at[half], square_recv_sem.at[half]).wait()
        square = send_square[half]
        for step in range(1, ranks):
            square = square + recv_square[half, step - 1]
        factor = lax.rsqrt(square / (channels * ranks) + 1e-06)
        for line in range(half_tokens // 128):
            column = jnp.sum(jnp.where(eye, factor[line : line + 1], 0.0), axis=1, keepdims=True)
            spread = jnp.broadcast_to(column, (128, DH))
            first = half * half_tokens + line * 128
            for head in range(heads):
                out_ref[first : first + 128, lanes(head)] = (
                    mixed[head, first : first + 128] * spread
                ).astype(jnp.bfloat16)

    for group in range(groups):
        whole(recv_slices.at[group], prefix_recv_sem.at[group]).wait()
        for member in range(GROUP):
            head = group * GROUP + member
            first = member // UNITS * (DH // TILE)
            carried = prefix[group, first : first + DH // TILE, member % UNITS]
            carried = carried.reshape(DH, DH).astype(jnp.float32)
            for chunk in range(chunks):
                block = slice(head % 2 * DH, (head % 2 + 1) * DH)
                states[head // 2, chunk, block, block] = (
                    carried + part_state[head, chunk]
                ).astype(jnp.bfloat16)
        for chunk in range(chunks):
            outer(group, chunk)
            if group == groups - 1 and (chunk + 1) * CHUNK % half_tokens == 0:
                half = (chunk + 1) * CHUNK // half_tokens - 1
                for step in range(1, ranks):
                    square_copy(half, step).start()
    for half in range(HALVES):
        finish(half)

    for half in range(HALVES):
        whole(recv_square.at[half], square_send_sem.at[half]).wait()
    for group in range(groups):
        whole(recv_slices.at[group], slice_send_sem.at[group]).wait()
        whole(recv_slices.at[group], prefix_send_sem.at[group]).wait()
        for other in range(1, slabs):

            @pl.when(other > slab)
            def _():
                total_copy(group, other).wait_send()

    @pl.when(ctx < ctx_count - 1)
    def _():
        halo_copy.wait_send()


def body(query_raw, key_raw, value_raw, gate_raw, conv_weight, norm_gain):
    tokens, channels = query_raw.shape
    heads = channels // DH
    chunks = tokens // CHUNK
    groups = heads // GROUP
    slabs = lax.axis_size("ctx") // SLAB
    ranks = lax.axis_size("head")
    dma = pltpu.SemaphoreType.DMA
    return pl.pallas_call(
        functools.partial(kernel, (heads, tokens, slabs, ranks)),
        out_shape=pltpu.VMEM((tokens, channels), jnp.bfloat16),
        in_specs=[pl.BlockSpec(memory_space=pltpu.HBM)] * 6,
        out_specs=pl.BlockSpec(memory_space=pltpu.VMEM),
        scratch_shapes=[
            pltpu.VMEM((4, heads, tokens, DH), jnp.bfloat16),
            pltpu.VMEM((3, KW, channels), jnp.float32),
            pltpu.VMEM((heads, DH), jnp.float32),
            pltpu.VMEM((3, heads, tokens, DH), jnp.bfloat16),
            pltpu.VMEM((3, TILE, channels), jnp.bfloat16),
            pltpu.VMEM((TILE, channels), jnp.bfloat16),
            pltpu.VMEM((TILE, channels), jnp.bfloat16),
            pltpu.VMEM((2, heads, (KW - 1) * SUBLANES + RIM, DH), jnp.float32),
            pltpu.VMEM((heads, DH, DH), jnp.float32),
            pltpu.VMEM((CHUNK, CHUNK), jnp.bfloat16),
            pltpu.VMEM((CHUNK, CHUNK), jnp.bfloat16),
            pltpu.VMEM((heads, tokens, DH), jnp.float32),
            pltpu.VMEM((heads, tokens, DH), jnp.float32),
            pltpu.VMEM((heads, chunks, DH, DH), jnp.float32),
            pltpu.VMEM((heads // 2, chunks, 2 * DH, 2 * DH), jnp.bfloat16),
            pltpu.VMEM((tokens, DH), jnp.float32),
            pltpu.VMEM((groups, SLAB, UNITS, TILE, DH), jnp.bfloat16),
            pltpu.VMEM((groups, SLAB - 1, UNITS, TILE, DH), jnp.bfloat16),
            pltpu.VMEM((groups, SLAB, UNITS, TILE, DH), jnp.float32),
            pltpu.VMEM((groups, UNITS, TILE, DH), jnp.bfloat16),
            pltpu.VMEM((groups, slabs, UNITS, TILE, DH), jnp.bfloat16),
            pltpu.VMEM((groups, SLAB, UNITS, TILE, DH), jnp.bfloat16),
            pltpu.VMEM((groups, SLAB, UNITS, TILE, DH), jnp.bfloat16),
            pltpu.VMEM((HALVES, 8, 128), jnp.float32),
            pltpu.VMEM((HALVES, ranks - 1, 8, 128), jnp.float32),
            dma((4, heads)),
            dma((2,)),
            dma((3,)),
            dma,
            dma,
            dma((groups,)),
            dma((groups,)),
            dma((groups, slabs)),
            dma((groups, slabs)),
            dma((groups,)),
            dma((groups,)),
            dma((HALVES,)),
            dma((HALVES,)),
            pltpu.SemaphoreType.REGULAR,
        ],
        compiler_params=pltpu.CompilerParams(
            collective_id=0, has_side_effects=True, vmem_limit_bytes=48 * 2**20
        ),
    )(
        *(
            pltpu.with_memory_space_constraint(item, pltpu.HBM)
            for item in (
                query_raw,
                key_raw,
                value_raw,
                gate_raw,
                conv_weight,
                norm_gain.reshape(heads, DH),
            )
        )
    )


def solution(mesh):
    placed = (
        P("ctx", "head"),
        P("ctx", "head"),
        P("ctx", "head"),
        P("ctx", "head"),
        P(None, None, "head"),
        P("head"),
    )
    return jax.shard_map(
        body, mesh=mesh, in_specs=placed, out_specs=P("ctx", "head"), check_vma=False
    )
```

```python
import functools

import jax
import jax.numpy as jnp
from jax import lax
from jax.experimental import pallas as pl
from jax.experimental.pallas import tpu as pltpu
from jax.sharding import PartitionSpec as P

DH = 128
KW = 4
CHUNK = 256
STRIP = 64
TILE = 16
SLAB = 16
GROUP = 4
UNITS = GROUP * (DH // TILE) // SLAB
SUBLANES = 8
STRIDE = CHUNK // SUBLANES
RIM = 32
HALVES = 2
MESH = pl.DeviceIdType.MESH
FAR_FIRST = sorted(range(1, SLAB), key=lambda step: (-min(step % 8, 8 - step % 8), -step))


def conv_rows(extended, taps):
    behind = pltpu.roll(extended, 1, 0)
    near = taps[3] * extended + taps[2] * behind
    far = taps[1] * extended + taps[0] * behind
    return (near + pltpu.roll(far, 2, 0))[8:]


def kernel(
    sizes,
    q_hbm,
    k_hbm,
    v_hbm,
    g_hbm,
    taps_hbm,
    gain_hbm,
    out_ref,
    raw,
    taps_ref,
    gain_ref,
    cooked,
    tails,
    tail_pack,
    halo,
    rim,
    later_state,
    stride_order,
    causal,
    mixed,
    gates,
    part_state,
    states,
    squares,
    send_slices,
    recv_slices,
    before,
    send_total,
    recv_total,
    send_prefix,
    prefix,
    send_square,
    recv_square,
    load_sem,
    small_sem,
    tail_sem,
    halo_send_sem,
    halo_recv_sem,
    slice_send_sem,
    slice_recv_sem,
    total_send_sem,
    total_recv_sem,
    prefix_send_sem,
    prefix_recv_sem,
    square_send_sem,
    square_recv_sem,
    ready,
):
    heads, tokens, slabs, ranks = sizes
    channels = heads * DH
    chunks = tokens // CHUNK
    groups = heads // GROUP
    ctx = lax.axis_index("ctx")
    rank = lax.axis_index("head")
    slab = ctx // SLAB
    place = lax.rem(ctx, SLAB)
    ctx_count = slabs * SLAB

    sources = (k_hbm, v_hbm, q_hbm, g_hbm)

    def load(array, head):
        return pltpu.make_async_copy(
            sources[array].at[:, pl.ds(pl.multiple_of(head * DH, DH), DH)],
            raw.at[array, head],
            load_sem.at[array, head],
        )

    barrier = pltpu.get_barrier_semaphore()

    def greet(target_ctx, target_rank):
        pl.semaphore_signal(
            barrier, inc=1, device_id=(target_ctx, target_rank), device_id_type=MESH
        )

    def load_tail(array):
        return pltpu.make_async_copy(
            sources[array].at[pl.ds(tokens - TILE, TILE), :], tails.at[array], tail_sem.at[array]
        )

    load_taps = pltpu.make_async_copy(taps_hbm, taps_ref, small_sem.at[0])
    load_gain = pltpu.make_async_copy(gain_hbm, gain_ref, small_sem.at[1])
    def start_pair(first, pair):
        for head in (2 * pair, 2 * pair + 1):
            load(first, head).start()
            load(first + 1, head).start()

    load_taps.start()
    start_pair(0, 0)
    start_pair(0, 1)
    for array in range(3):
        load_tail(array).start()

    for step in range(1, SLAB):
        greet(slab * SLAB + lax.rem(place + step, SLAB), rank)
    for step in range(1, ranks):
        greet(ctx, lax.rem(rank + step, ranks))

    @pl.when(ctx > 0)
    def _():
        greet(ctx - 1, rank)

    @pl.when(ctx < ctx_count - 1)
    def _():
        greet(ctx + 1, rank)

    for other in range(1, slabs):

        @pl.when(other > slab)
        def _():
            greet(other * SLAB + place, rank)

    row = lax.broadcasted_iota(jnp.int32, (CHUNK, CHUNK), 0)
    column = lax.broadcasted_iota(jnp.int32, (CHUNK, CHUNK), 1)

    def token_of(position):
        return position % SUBLANES * STRIDE + position // SUBLANES

    stride_order[...] = jnp.where(column == token_of(row), 1.0, 0.0).astype(jnp.bfloat16)
    causal[...] = jnp.where(row >= token_of(column), 1.0, 0.0).astype(jnp.bfloat16)

    halo_copy = pltpu.make_async_remote_copy(
        src_ref=tail_pack,
        dst_ref=halo,
        send_sem=halo_send_sem,
        recv_sem=halo_recv_sem,
        device_id=(ctx + 1, rank),
        device_id_type=MESH,
    )

    def lanes(head):
        return slice(head * DH, (head + 1) * DH)

    def taps_of(kind, head, factor):
        return [taps_ref[kind, j : j + 1, lanes(head)] * factor for j in range(KW)]

    first_sublane = lax.broadcasted_iota(jnp.int32, (SUBLANES, DH), 0) == 0

    def last_rows(rows):
        return [
            pltpu.roll(rows[CHUNK + (j - 3) * SUBLANES :][:SUBLANES], 1, 0) for j in range(KW - 1)
        ]

    def conv_strided(extended, taps):
        count = extended.shape[0] - (KW - 1) * SUBLANES
        terms = [taps[j] * extended[j * SUBLANES : j * SUBLANES + count] for j in range(KW)]
        return (terms[3] + terms[2]) + (terms[1] + terms[0])

    def cook(array, head, rows, extended):
        if array == 0:
            half = conv_strided(extended, taps_of(1, head, 0.5))
            cooked[0, head, rows] = (half + half * jnp.tanh(half)).astype(jnp.bfloat16)
        else:
            cooked[1, head, rows] = conv_strided(extended, taps_of(2, head, 1.0)).astype(
                jnp.bfloat16
            )

    def in_stride_order(array, pair, chunk):
        rows = slice(chunk * CHUNK, (chunk + 1) * CHUNK)
        both = jnp.concatenate([raw[array, 2 * pair, rows], raw[array, 2 * pair + 1, rows]], axis=1)
        return jnp.dot(stride_order[...], both, preferred_element_type=jnp.float32)

    def keys_values(pair):
        behind = None
        for chunk in range(chunks):
            rows_of = [in_stride_order(array, pair, chunk) for array in range(2)]
            last = [last_rows(item) for item in rows_of]
            for member in range(2):
                head = 2 * pair + member
                here = slice(member * DH, (member + 1) * DH)
                for array in range(2):
                    rows = rows_of[array][:, here]
                    edge = [item[:, here] for item in last[array]]
                    if chunk == 0:
                        rim[array, head] = jnp.concatenate(edge + [rows[:RIM]], axis=0)
                        cook(
                            array,
                            head,
                            slice(RIM, CHUNK),
                            rows[RIM - (KW - 1) * SUBLANES :],
                        )
                    else:
                        edge = [
                            jnp.where(first_sublane, before_it[:, here], after_it)
                            for before_it, after_it in zip(behind[array], edge)
                        ]
                        cook(
                            array,
                            head,
                            slice(chunk * CHUNK, (chunk + 1) * CHUNK),
                            jnp.concatenate(edge + [rows], axis=0),
                        )
            behind = last

    def finish_rim(head):
        arrived = halo[:, lanes(head)].astype(jnp.float32)
        for array in range(2):
            edge = [
                jnp.where(
                    first_sublane,
                    arrived[array * 3 + j : array * 3 + j + 1],
                    rim[array, head, j * SUBLANES : (j + 1) * SUBLANES],
                )
                for j in range(KW - 1)
            ]
            rows = rim[array, head, (KW - 1) * SUBLANES :]
            cook(array, head, slice(0, RIM), jnp.concatenate(edge + [rows], axis=0))

    def product(head, chunk):
        rows = slice(chunk * CHUNK, (chunk + 1) * CHUNK)
        part_state[head, chunk] = lax.dot_general(
            cooked[0, head, rows],
            cooked[1, head, rows],
            (((0,), (0,)), ((), ())),
            preferred_element_type=jnp.float32,
        )

    def pack_tails():
        wide = lax.broadcasted_iota(jnp.int32, (TILE, channels), 0)
        key, value, query = [
            pltpu.roll(tails[array].astype(jnp.float32), 3 * (array + 1), 0) for array in range(3)
        ]
        packed = jnp.where(wide < 3, key, jnp.where(wide < 6, value, query))
        tail_pack[...] = packed.astype(jnp.bfloat16)

    def extended_rows(array, head, row):
        if row == 0:
            ahead = halo[:, lanes(head)].astype(jnp.float32)
            own = raw[array, head, 0:STRIP, :]
            return jnp.concatenate(
                [pltpu.roll(ahead, TILE - 1, 0)[:SUBLANES], own.astype(jnp.float32)], axis=0
            )
        return raw[array, head, row - TILE : row + STRIP, :].astype(jnp.float32)[8:]

    def sum_later(head):
        total = part_state[head, 1]
        for chunk in range(2, chunks):
            total = total + part_state[head, chunk]
        later_state[head] = total

    def finish_state(head, group, member):
        rounded = (part_state[head, 0] + later_state[head]).astype(jnp.bfloat16)
        for piece in range(DH // TILE):
            owner = member // UNITS * (DH // TILE) + piece
            send_slices[group, owner, member % UNITS] = rounded[piece * TILE : (piece + 1) * TILE]

    def chunk_prefixes(head):
        running = part_state[head, 0]
        for chunk in range(1, chunks):
            own = part_state[head, chunk]
            part_state[head, chunk] = running
            running = running + own
        part_state[head, 0] = jnp.zeros((DH, DH), jnp.float32)

    def peer(step):
        return lax.rem(place + step, SLAB)

    def slice_copy(group, step):
        return pltpu.make_async_remote_copy(
            src_ref=send_slices.at[group, peer(step)],
            dst_ref=recv_slices.at[group, step - 1],
            send_sem=slice_send_sem.at[group],
            recv_sem=slice_recv_sem.at[group],
            device_id=(slab * SLAB + peer(step), rank),
            device_id_type=MESH,
        )

    def total_copy(group, other):
        return pltpu.make_async_remote_copy(
            src_ref=send_total.at[group],
            dst_ref=recv_total.at[group, slab],
            send_sem=total_send_sem.at[group, other],
            recv_sem=total_recv_sem.at[group, slab],
            device_id=(other * SLAB + place, rank),
            device_id_type=MESH,
        )

    def total_arrival(group, other):
        return pltpu.make_async_remote_copy(
            src_ref=send_total.at[group],
            dst_ref=recv_total.at[group, other],
            send_sem=total_send_sem.at[group, other],
            recv_sem=total_recv_sem.at[group, other],
            device_id=(other * SLAB + place, rank),
            device_id_type=MESH,
        )

    def prefix_copy(group, step):
        return pltpu.make_async_remote_copy(
            src_ref=send_prefix.at[group, peer(step)],
            dst_ref=prefix.at[group, place],
            send_sem=prefix_send_sem.at[group],
            recv_sem=prefix_recv_sem.at[group],
            device_id=(slab * SLAB + peer(step), rank),
            device_id_type=MESH,
        )

    def whole(ref, sem):
        return pltpu.make_async_copy(ref, ref, sem)

    def send_states(group):
        for step in FAR_FIRST:
            slice_copy(group, step).start()

    def sum_slab(group):
        whole(recv_slices.at[group], slice_recv_sem.at[group]).wait()
        total = send_slices[group, place].astype(jnp.float32)
        for step in range(1, SLAB):
            total = total + recv_slices[group, step - 1].astype(jnp.float32)
        send_total[group] = total.astype(jnp.bfloat16)
        if group == 0:

            @pl.when(slab < slabs - 1)
            def _():
                pl.semaphore_wait(ready, slabs - 1 - slab)

        for other in range(slabs - 1, 0, -1):

            @pl.when(other > slab)
            def _():
                total_copy(group, other).start()

    def sum_before(group):
        running = jnp.zeros((UNITS, TILE, DH), jnp.float32)
        for index in range(SLAB):
            before[group, index] = running
            if index < SLAB - 1:
                step = lax.rem(place - index + SLAB, SLAB)
                got = recv_slices[group, jnp.maximum(step - 1, 0)].astype(jnp.float32)
                own = send_slices[group, place].astype(jnp.float32)
                running = running + jnp.where(step == 0, own, got)

    def send_prefixes(group):
        def add(other, total):
            total_arrival(group, other).wait_recv()
            return total + recv_total[group, other].astype(jnp.float32)

        earlier = lax.fori_loop(0, slab, add, jnp.zeros((UNITS, TILE, DH), jnp.float32))
        for index in range(SLAB):
            send_prefix[group, index] = (earlier + before[group, index]).astype(jnp.bfloat16)
        for step in FAR_FIRST:
            prefix_copy(group, step).start()
        prefix[group, place] = send_prefix[group, place]

    def queries(head):
        query_taps = taps_of(0, head, 0.5)
        for row in range(0, tokens, STRIP):
            half = conv_rows(extended_rows(2, head, row), query_taps)
            scaled = half * DH ** (-0.5)
            cooked[2, head, row : row + STRIP, :] = (scaled + scaled * jnp.tanh(half)).astype(
                jnp.bfloat16
            )

    def inner(head):
        for chunk in range(chunks):
            rows = slice(chunk * CHUNK, (chunk + 1) * CHUNK)
            scores = lax.dot_general(
                cooked[2, head, rows],
                cooked[0, head, rows],
                (((1,), (1,)), ((), ())),
                preferred_element_type=jnp.float32,
            )
            weights = scores.astype(jnp.bfloat16) * causal[...]
            here = jnp.dot(weights, cooked[1, head, rows], preferred_element_type=jnp.float32)
            if chunk > 0:
                here = here + jnp.dot(
                    cooked[2, head, rows],
                    part_state[head, chunk].astype(jnp.bfloat16),
                    preferred_element_type=jnp.float32,
                )
            mixed[head, rows] = here

    def gate(head):
        gain = gain_ref[pl.ds(head, 1), :] * 0.5
        for row in range(0, tokens, STRIP):
            half = raw[3, head, row : row + STRIP, :].astype(jnp.float32) * 0.5
            gates[head, row : row + STRIP, :] = gain + gain * jnp.tanh(half)

    pairs = heads // 2

    def pair_loads(array, pair):
        load(array, 2 * pair).wait()
        load(array, 2 * pair + 1).wait()

    load_taps.wait()
    for pair in range(pairs // 2):
        pair_loads(0, pair)
        pair_loads(1, pair)
        start_pair(0, pair + 2)
        keys_values(pair)

    for array in range(3):
        load_tail(array).wait()
    pack_tails()
    pl.semaphore_wait(
        barrier,
        SLAB - 1 + ranks - 1 + slab + jnp.minimum(ctx, 1) + jnp.minimum(ctx_count - 1 - ctx, 1),
    )

    @pl.when(ctx < ctx_count - 1)
    def _():
        halo_copy.start()

    for other in range(slabs - 1):

        @pl.when(other < slab)
        def _():
            pl.semaphore_signal(
                ready, inc=1, device_id=(other * SLAB + place, rank), device_id_type=MESH
            )

    load_gain.start()
    for pair in range(pairs // 2, pairs):
        pair_loads(0, pair)
        pair_loads(1, pair)
        start_pair(2, 2 * pair - pairs)
        start_pair(2, 2 * pair - pairs + 1)
        keys_values(pair)
    for head in range(heads):
        for chunk in range(1, chunks):
            product(head, chunk)
        sum_later(head)

    @pl.when(ctx == 0)
    def _():
        halo[...] = jnp.zeros_like(halo)

    @pl.when(ctx > 0)
    def _():
        halo_copy.wait_recv()

    for group in range(groups):
        for member in range(GROUP):
            finish_rim(group * GROUP + member)
        for member in range(GROUP):
            product(group * GROUP + member, 0)
            finish_state(group * GROUP + member, group, member)
        send_states(group)

    load_gain.wait()
    for head in range(heads):
        chunk_prefixes(head)
    for head in range(heads):
        load(2, head).wait()
        load(3, head).wait()

    def query_part(first, last):
        for head in range(first, last):
            queries(head)
            inner(head)
            gate(head)

    query_part(0, heads - 2)
    for group in range(groups):
        sum_slab(group)
    for group in range(groups):
        sum_before(group)
    query_part(heads - 2, heads)
    states[...] = jnp.zeros_like(states)
    send_square[...] = jnp.zeros_like(send_square)
    for group in range(groups):
        send_prefixes(group)

    eye = (
        lax.broadcasted_iota(jnp.int32, (128, 128), 0)
        == lax.broadcasted_iota(jnp.int32, (128, 128), 1)
    )
    half_tokens = tokens // HALVES

    def square_copy(half, step):
        return pltpu.make_async_remote_copy(
            src_ref=send_square.at[half],
            dst_ref=recv_square.at[half, step - 1],
            send_sem=square_send_sem.at[half],
            recv_sem=square_recv_sem.at[half],
            device_id=(ctx, lax.rem(rank + step, ranks)),
            device_id_type=MESH,
        )

    def outer(group, chunk):
        rows = slice(chunk * CHUNK, (chunk + 1) * CHUNK)
        total = None
        for pair in range(group * GROUP // 2, (group + 1) * GROUP // 2):
            both = jnp.concatenate(
                [cooked[2, 2 * pair, rows], cooked[2, 2 * pair + 1, rows]], axis=1
            )
            carried = jnp.dot(both, states[pair], preferred_element_type=jnp.float32)
            for member in range(2):
                head = 2 * pair + member
                here = mixed[head, rows] + carried[:, member * DH : (member + 1) * DH]
                mixed[head, rows] = here * gates[head, rows]
                total = here * here if total is None else total + here * here
        if group > 0:
            total = total + squares[rows]
        if group < groups - 1:
            squares[rows] = total
            return
        column = jnp.sum(total, axis=1, keepdims=True)
        for part in range(CHUNK // 128):
            index = chunk * (CHUNK // 128) + part
            half, line = index // (half_tokens // 128), index % (half_tokens // 128)
            send_square[half, line : line + 1, :] = jnp.sum(
                jnp.where(eye, column[part * 128 : (part + 1) * 128], 0.0), axis=0, keepdims=True
            )

    def finish(half):
        whole(recv_square.at[half], square_recv_sem.at[half]).wait()
        square = send_square[half]
        for step in range(1, ranks):
            square = square + recv_square[half, step - 1]
        factor = lax.rsqrt(square / (channels * ranks) + 1e-06)
        for line in range(half_tokens // 128):
            column = jnp.sum(jnp.where(eye, factor[line : line + 1], 0.0), axis=1, keepdims=True)
            spread = jnp.broadcast_to(column, (128, DH))
            first = half * half_tokens + line * 128
            for head in range(heads):
                out_ref[first : first + 128, lanes(head)] = (
                    mixed[head, first : first + 128] * spread
                ).astype(jnp.bfloat16)

    for group in range(groups):
        whole(recv_slices.at[group], prefix_recv_sem.at[group]).wait()
        for member in range(GROUP):
            head = group * GROUP + member
            first = member // UNITS * (DH // TILE)
            carried = prefix[group, first : first + DH // TILE, member % UNITS]
            block = slice(head % 2 * DH, (head % 2 + 1) * DH)
            states[head // 2, block, block] = carried.reshape(DH, DH)
        for chunk in range(chunks):
            outer(group, chunk)
            if group == groups - 1 and (chunk + 1) * CHUNK % half_tokens == 0:
                half = (chunk + 1) * CHUNK // half_tokens - 1
                for step in range(1, ranks):
                    square_copy(half, step).start()
    for half in range(HALVES):
        finish(half)

    for half in range(HALVES):
        whole(recv_square.at[half], square_send_sem.at[half]).wait()
    for group in range(groups):
        whole(recv_slices.at[group], slice_send_sem.at[group]).wait()
        whole(recv_slices.at[group], prefix_send_sem.at[group]).wait()
        for other in range(1, slabs):

            @pl.when(other > slab)
            def _():
                total_copy(group, other).wait_send()

    @pl.when(ctx < ctx_count - 1)
    def _():
        halo_copy.wait_send()


def body(query_raw, key_raw, value_raw, gate_raw, conv_weight, norm_gain):
    tokens, channels = query_raw.shape
    heads = channels // DH
    chunks = tokens // CHUNK
    groups = heads // GROUP
    slabs = lax.axis_size("ctx") // SLAB
    ranks = lax.axis_size("head")
    dma = pltpu.SemaphoreType.DMA
    return pl.pallas_call(
        functools.partial(kernel, (heads, tokens, slabs, ranks)),
        out_shape=pltpu.VMEM((tokens, channels), jnp.bfloat16),
        in_specs=[pl.BlockSpec(memory_space=pltpu.HBM)] * 6,
        out_specs=pl.BlockSpec(memory_space=pltpu.VMEM),
        scratch_shapes=[
            pltpu.VMEM((4, heads, tokens, DH), jnp.bfloat16),
            pltpu.VMEM((3, KW, channels), jnp.float32),
            pltpu.VMEM((heads, DH), jnp.float32),
            pltpu.VMEM((3, heads, tokens, DH), jnp.bfloat16),
            pltpu.VMEM((3, TILE, channels), jnp.bfloat16),
            pltpu.VMEM((TILE, channels), jnp.bfloat16),
            pltpu.VMEM((TILE, channels), jnp.bfloat16),
            pltpu.VMEM((2, heads, (KW - 1) * SUBLANES + RIM, DH), jnp.float32),
            pltpu.VMEM((heads, DH, DH), jnp.float32),
            pltpu.VMEM((CHUNK, CHUNK), jnp.bfloat16),
            pltpu.VMEM((CHUNK, CHUNK), jnp.bfloat16),
            pltpu.VMEM((heads, tokens, DH), jnp.float32),
            pltpu.VMEM((heads, tokens, DH), jnp.float32),
            pltpu.VMEM((heads, chunks, DH, DH), jnp.float32),
            pltpu.VMEM((heads // 2, 2 * DH, 2 * DH), jnp.bfloat16),
            pltpu.VMEM((tokens, DH), jnp.float32),
            pltpu.VMEM((groups, SLAB, UNITS, TILE, DH), jnp.bfloat16),
            pltpu.VMEM((groups, SLAB - 1, UNITS, TILE, DH), jnp.bfloat16),
            pltpu.VMEM((groups, SLAB, UNITS, TILE, DH), jnp.float32),
            pltpu.VMEM((groups, UNITS, TILE, DH), jnp.bfloat16),
            pltpu.VMEM((groups, slabs, UNITS, TILE, DH), jnp.bfloat16),
            pltpu.VMEM((groups, SLAB, UNITS, TILE, DH), jnp.bfloat16),
            pltpu.VMEM((groups, SLAB, UNITS, TILE, DH), jnp.bfloat16),
            pltpu.VMEM((HALVES, 8, 128), jnp.float32),
            pltpu.VMEM((HALVES, ranks - 1, 8, 128), jnp.float32),
            dma((4, heads)),
            dma((2,)),
            dma((3,)),
            dma,
            dma,
            dma((groups,)),
            dma((groups,)),
            dma((groups, slabs)),
            dma((groups, slabs)),
            dma((groups,)),
            dma((groups,)),
            dma((HALVES,)),
            dma((HALVES,)),
            pltpu.SemaphoreType.REGULAR,
        ],
        compiler_params=pltpu.CompilerParams(
            collective_id=0, has_side_effects=True, vmem_limit_bytes=48 * 2**20
        ),
    )(
        *(
            pltpu.with_memory_space_constraint(item, pltpu.HBM)
            for item in (
                query_raw,
                key_raw,
                value_raw,
                gate_raw,
                conv_weight,
                norm_gain.reshape(heads, DH),
            )
        )
    )


def solution(mesh):
    placed = (
        P("ctx", "head"),
        P("ctx", "head"),
        P("ctx", "head"),
        P("ctx", "head"),
        P(None, None, "head"),
        P("head"),
    )
    return jax.shard_map(
        body, mesh=mesh, in_specs=placed, out_specs=P("ctx", "head"), check_vma=False
    )
```
